32 devices in a mesh: row: 4 (over z), col: 8 (over y, x, core).
Axes of the slice: x: 2, y: 2, z: 4, core: 2. Of those that a mesh axis runs over, the one named last changes fastest.
Arguments:
- tokens: bfloat16 [2560, 8192], P('row', 'col'), may hold values from -6 to 6
- norm_gain: bfloat16 [8192], replicated, may hold values from 0.099609375 to 1.8984375
- w_query: bfloat16 [8192, 8192], P('row', 'col')
- w_key: bfloat16 [8192, 1024], P('row')
- w_value: bfloat16 [8192, 1024], P('row'), may hold values from -0.0625 to 0.0625
- w_out: bfloat16 [8192, 8192], P('row', 'col'), may hold values from -0.0625 to 0.0625
- doc_lengths: int32 [4], replicated, may hold values from 1 to 1280, 2560 in all
Outputs:
- layer_out: bfloat16 [2560, 8192], P('row', 'col')
The draws below stay inside these ranges and needn't reach their ends.
Inputs may be any that keep to these rules, and one draw needn't show every extreme that they name: `doc_lengths`: positive lengths that add up to 2560; the largest is exactly 1280.
All inputs are finite; a program needn't handle non-finite values.
Results may differ from the reference program's by a relative error of at most 0.011.
Values may be sent and summed in bfloat16 or wider, within the bound.
No kernel may reach another device: no remote copies, remote signals or barrier semaphores. Data moves between devices by JAX's collectives and lax.ppermute only.
A program may use at most 192 MiB of HBM per device.

```python
import math
import jax
import jax.numpy as jnp
import numpy as np
from jax import lax

D = 8192
HEADS = 64
KVH = 8
HD = 128
DOCS = 4
TOKENS = 2560


def query_matrix(key):
    return jax.random.normal(jax.random.fold_in(key, 7), (D, HEADS * HD), jnp.float32) * D ** (-0.5)


def draw_w_query(key, part):
    return query_matrix(key).astype(jnp.bfloat16)


def draw_w_key(key, part):
    noise = jax.random.normal(jax.random.fold_in(key, 8), (D, KVH, HD), jnp.float32) * D ** (-0.5)
    result = noise
    return result.reshape(D, KVH * HD).astype(jnp.bfloat16)


def level_of(stream_key, shape, cuts, smallest, largest):
    gain, own = 1.0, jax.random.fold_in(stream_key, 6)
    for position, blocks in cuts:
        heights = jnp.exp(jax.random.uniform(jax.random.fold_in(own, position), (blocks,), jnp.float32, smallest / len(cuts), largest / len(cuts)))
        gain = gain * jnp.repeat(heights, shape[position] // blocks).reshape([-1 if axis == position else 1 for axis in range(len(shape))])
    return gain


def split_up(number_of, total, limit, slope):
    loads = [(1 << 20) // math.isqrt(standing ** slope) + 1 for standing in range(2, number_of + 1)]
    spare, given = total - limit - (number_of - 1), [1] * (number_of - 1)
    while spare > 0:
        candidates = [i for i in range(number_of - 1) if given[i] < limit]
        pool, budget = sum([loads[i] for i in candidates]), spare
        for i in candidates:
            more = min(limit - given[i], max(1, budget * loads[i] // pool), spare)
            given[i] = given[i] + more
            spare = spare - more
    return np.array([limit] + given)


def uneven(stream_key, count, total, most, slope):
    if count == 2:
        one = jax.random.randint(stream_key, (), max(1, total - most), min(most, total - 1) + 1)
        return jnp.stack([one, total - one])
    tallies = jnp.asarray(split_up(count, total, most, slope), jnp.int32)
    pairs = (count - 1) // 2
    donor, sink = tallies[1:1 + 2 * pairs:2], tallies[2:2 + 2 * pairs:2]
    room = jnp.minimum(donor - 1, most - sink)
    shifted = jax.random.randint(jax.random.fold_in(stream_key, 1), (pairs,), 0, 1 << 20) % (room + 1)
    tallies = tallies.at[1:1 + 2 * pairs:2].set(donor - shifted).at[2:2 + 2 * pairs:2].set(sink + shifted)
    return tallies[jax.random.permutation(jax.random.fold_in(stream_key, 2), count)]


def scatter_about(key, shape, scale, most, pieces=(), held_as=jnp.bfloat16):
    loudness = level_of(key, shape, pieces, -0.22, 0.18) if pieces else 1.0
    values = jax.random.normal(key, shape, jnp.float32) * scale * loudness
    return jnp.minimum(jnp.maximum(values, -most), most).astype(held_as)


def setup_inputs(seed: int = 0) -> dict:
    key_of = jax.random.split(jax.random.key(seed), 8)
    tokens = scatter_about(key_of[0], (TOKENS, D), 1.0, 6.0, ((0, 4), (1, 8)))
    norm_gain = jnp.clip(1.0 + 0.18 * jax.random.normal(key_of[1], (D,), jnp.float32), 0.099609375, 1.8984375).astype(jnp.bfloat16)
    w_query = draw_w_query(jax.random.fold_in(key_of[7], 71), 0)
    w_key = draw_w_key(jax.random.fold_in(key_of[7], 71), 0)
    w_value = scatter_about(key_of[4], (D, KVH * HD), D ** -0.5, 0.0625, ((0, 4),))
    w_out = scatter_about(key_of[5], (HEADS * HD, D), (HEADS * HD) ** -0.5, 0.0625, ((0, 4), (1, 8)))
    doc_lengths = uneven(key_of[6], DOCS, TOKENS, TOKENS // 2, 0).astype(jnp.int32)
    return dict(tokens=tokens, norm_gain=norm_gain, w_query=w_query, w_key=w_key, w_value=w_value, w_out=w_out, doc_lengths=doc_lengths)


rope_base = 500000.0
norm_eps = 1e-05
masked_value = -1e+30

def rope_tables(positions, head_dim):
    freq_index = jnp.arange(head_dim // 2, dtype=jnp.int32).astype(jnp.float32)
    inverse = rope_base ** (-2.0 * freq_index / head_dim)
    angles = positions.astype(jnp.float32)[:, None] * inverse[None, :]
    return (jnp.cos(angles), jnp.sin(angles))

def rotate(vectors, cosine, sine):
    half_dim = vectors.shape[-1] // 2
    first = vectors[..., :half_dim]
    second = vectors[..., half_dim:]
    cos_part = cosine[:, None, :]
    sin_part = sine[:, None, :]
    return jnp.concatenate([first * cos_part - second * sin_part, second * cos_part + first * sin_part], axis=-1)

def doc_index(positions, doc_ends):
    return lax.optimization_barrier(jnp.sum((positions[:, None] >= doc_ends[None, :]).astype(jnp.int32), axis=1))

def reference(tokens, norm_gain, w_query, w_key, w_value, w_out, doc_lengths):
    whole_f = tokens.astype(jnp.float32)
    inv_rms = lax.rsqrt(lax.optimization_barrier(jnp.mean(whole_f * whole_f, axis=1, keepdims=True)) + norm_eps)
    normed = (whole_f * inv_rms * norm_gain.astype(jnp.float32)[None, :]).astype(jnp.bfloat16)
    queries = jnp.dot(normed, w_query, preferred_element_type=jnp.float32).reshape(TOKENS, HEADS, HD)
    keys_f = jnp.dot(normed, w_key, preferred_element_type=jnp.float32).reshape(TOKENS, KVH, HD)
    values_b = jnp.dot(normed, w_value, preferred_element_type=jnp.float32).astype(jnp.bfloat16).reshape(TOKENS, KVH, HD)
    positions = jnp.arange(TOKENS, dtype=jnp.int32)
    cosine, sine = rope_tables(positions, HD)
    q_rot = rotate(queries, cosine, sine).astype(jnp.bfloat16)
    k_rot = rotate(keys_f, cosine, sine).astype(jnp.bfloat16)
    doc_ends = jnp.cumsum(doc_lengths).astype(jnp.int32)
    docs = doc_index(positions, doc_ends)
    allowed = (docs[:, None] == docs[None, :]) & (positions[None, :] <= positions[:, None])
    group_size = HEADS // KVH
    score_scale = HD ** (-0.5)

    def one_head(head):
        q_head = lax.dynamic_index_in_dim(q_rot, head, 1, keepdims=False)
        k_head = lax.dynamic_index_in_dim(k_rot, head // group_size, 1, keepdims=False)
        v_head = lax.dynamic_index_in_dim(values_b, head // group_size, 1, keepdims=False)
        scores = jnp.dot(q_head, k_head.T, preferred_element_type=jnp.float32) * score_scale
        masked = jnp.where(allowed, scores, masked_value)
        row_max = lax.optimization_barrier(jnp.max(masked, axis=1, keepdims=True))
        weights = jnp.where(allowed, jnp.exp(masked - row_max), 0.0)
        totals = lax.optimization_barrier(jnp.sum(weights, axis=1, keepdims=True))
        mixed = jnp.dot(weights.astype(jnp.bfloat16), v_head, preferred_element_type=jnp.float32)
        return (mixed / totals).astype(jnp.bfloat16)
    per_head = lax.map(one_head, jnp.arange(HEADS, dtype=jnp.int32))
    context = per_head.transpose(1, 0, 2).reshape(TOKENS, HEADS * HD)
    projected = jnp.dot(context, w_out, preferred_element_type=jnp.float32)
    return (whole_f + projected).astype(jnp.bfloat16)
```

```python
import functools

import jax
import jax.numpy as jnp
from jax import lax
from jax.experimental import pallas as pl
from jax.experimental.pallas import tpu as pltpu
from jax.sharding import PartitionSpec as P

HEADS = 64
KVH = 8
HD = 128


rope_base = 500000.0
norm_eps = 1e-05
masked_value = -1e30
f32 = jnp.float32
bf16 = jnp.bfloat16


def rope_tables(positions, head_dim):
    freq_index = jnp.arange(head_dim // 2, dtype=jnp.int32).astype(jnp.float32)
    inverse = rope_base ** (-2.0 * freq_index / head_dim)
    angles = positions.astype(jnp.float32)[:, None] * inverse[None, :]
    return (jnp.cos(angles), jnp.sin(angles))


def rotate(vectors, cosine, sine):
    half_dim = vectors.shape[-1] // 2
    first = vectors[..., :half_dim]
    second = vectors[..., half_dim:]
    cos_part = cosine[:, None, :]
    sin_part = sine[:, None, :]
    return jnp.concatenate(
        [first * cos_part - second * sin_part, second * cos_part + first * sin_part], axis=-1
    )


def running_sums(doc_lengths):
    ends, total = [], jnp.int32(0)
    for i in range(doc_lengths.shape[0]):
        total = total + doc_lengths[i]
        ends.append(total)
    return jnp.stack(ends)


def doc_index(positions, doc_ends):
    return jnp.sum((positions[:, None] >= doc_ends[None, :]).astype(jnp.int32), axis=1)


CHUNKS = 2
KEY_BLOCK = 256


def attention_kernel(first_of, tile_rows, rows_per_group, ends_ref, q_ref, k_ref, v_ref, o_ref):
    docs = ends_ref.shape[0]
    group = pl.program_id(0)
    first = group * rows_per_group + first_of
    queries = q_ref[0].reshape(2 * tile_rows, HD)
    row = lax.broadcasted_iota(jnp.int32, (2 * tile_rows, 1), 0)
    pos = first + jnp.where(row >= tile_rows, row - tile_rows, row)
    start = jnp.zeros_like(pos)
    low = jnp.int32(0)
    for e in range(docs - 1):
        end = ends_ref[e]
        start = jnp.where(pos >= end, end, start)
        low = jnp.where(first >= end, end, low)
    scale = HD ** (-0.5)

    def visit(block, state):
        run_max, run_total, run_acc = state
        at = pl.multiple_of(block * KEY_BLOCK, KEY_BLOCK)
        keys = k_ref[pl.ds(at, KEY_BLOCK), :]
        values = v_ref[pl.ds(at, KEY_BLOCK), :]
        scores = lax.dot_general(
            queries, keys, (((1,), (1,)), ((), ())), preferred_element_type=f32
        )
        key_pos = at + lax.broadcasted_iota(jnp.int32, (1, KEY_BLOCK), 1)
        allowed = (key_pos <= pos) & (key_pos >= start)
        masked = jnp.where(allowed, scores, masked_value)
        new_max = jnp.maximum(run_max, jnp.max(masked, axis=1, keepdims=True))
        factor = jnp.exp((run_max - new_max) * scale)
        weights = jnp.where(allowed, jnp.exp((masked - new_max) * scale), 0.0)
        new_total = run_total * factor + jnp.sum(weights, axis=1, keepdims=True)
        new_acc = run_acc * factor + jnp.dot(
            weights.astype(bf16), values, preferred_element_type=f32
        )
        return new_max, new_total, new_acc

    state = (
        jnp.full((2 * tile_rows, 1), masked_value, f32),
        jnp.zeros((2 * tile_rows, 1), f32),
        jnp.zeros((2 * tile_rows, HD), f32),
    )
    last = (first + tile_rows - 1) // KEY_BLOCK + 1
    run_max, run_total, run_acc = lax.fori_loop(low // KEY_BLOCK, last, visit, state)
    context = (run_acc / run_total).astype(bf16)
    o_ref[0, :, :HD] = context[:tile_rows]
    o_ref[0, :, HD:] = context[tile_rows:]


def attend(queries, keys, values, doc_ends, first_of, rows_per_group):
    groups, heads, tile_rows, _ = queries.shape
    total = keys.shape[0]
    return pl.pallas_call(
        functools.partial(attention_kernel, first_of, tile_rows, rows_per_group),
        grid=(groups,),
        in_specs=[
            pl.BlockSpec(memory_space=pltpu.SMEM),
            pl.BlockSpec((1, heads, tile_rows, HD), lambda g: (g, 0, 0, 0)),
            pl.BlockSpec((total, HD), lambda g: (0, 0)),
            pl.BlockSpec((total, HD), lambda g: (0, 0)),
        ],
        out_specs=pl.BlockSpec((1, tile_rows, heads * HD), lambda g: (g, 0, 0)),
        out_shape=jax.ShapeDtypeStruct((groups, tile_rows, heads * HD), bf16),
        compiler_params=pltpu.CompilerParams(vmem_limit_bytes=32 * 2**20),
        cost_estimate=pl.CostEstimate(
            flops=groups * heads * tile_rows * 1024 * HD * 4,
            bytes_accessed=4 * total * HD + 4 * groups * heads * tile_rows * HD,
            transcendentals=groups * heads * tile_rows * 1024,
        ),
    )(doc_ends, queries, keys, values)


def plane_pieces(own, core, cols):
    def swap(x, bit):
        return lax.ppermute(x, "col", [(i, i ^ bit) for i in range(cols)])

    along_x = swap(own, 2)
    along_y = swap(own, 4)
    partner = swap(own, 1)
    passed = jnp.where(core == 0, along_x, along_y)
    across = lax.ppermute(passed, "col", [(i, i ^ (2 if i & 1 else 4)) for i in range(cols)])
    return [
        own,
        partner,
        along_x,
        swap(along_x, 1),
        along_y,
        swap(along_y, 1),
        across,
        swap(across, 1),
    ]


def ring_sum(part_of, row_index, rows):
    onward = [(i, (i + 1) % rows) for i in range(rows)]
    total = part_of((row_index - 1) % rows)
    for step in range(1, rows):
        came = lax.ppermute(total.astype(bf16), "row", onward)
        total = came.astype(f32) + part_of((row_index - 1 - step) % rows)
    return total


def stationary_body(rows, cols, tokens, norm_gain, w_query, w_key, w_value, w_out, doc_lengths):
    tok_rows, feats = tokens.shape
    col = lax.axis_index("col")
    row = lax.axis_index("row")
    core = col % 2
    depth = w_query.shape[0]
    part = tok_rows // (CHUNKS * cols)
    tile_rows = part * cols
    total_tokens = tok_rows * rows
    pair = 2 * HD
    doc_ends = running_sums(doc_lengths)
    cosine, sine = rope_tables(jnp.arange(total_tokens, dtype=jnp.int32), HD)
    cos_all = jnp.concatenate([cosine, cosine], axis=1)
    sin_all = jnp.concatenate([-sine, sine], axis=1)

    def rope(vectors, cos_part, sin_part):
        half = HD // 2
        turned = jnp.concatenate([vectors[..., half:], vectors[..., :half]], axis=-1)
        return vectors * cos_part + turned * sin_part

    spread = tokens.reshape(CHUNKS, cols, part, feats).transpose(1, 0, 2, 3)
    mine = lax.all_to_all(spread, "col", 0, 0).astype(f32)
    rms = lax.rsqrt(jnp.mean(mine * mine, axis=(0, 3), keepdims=True) + norm_eps)
    gain = norm_gain.astype(f32).reshape(cols, 1, 1, feats)
    normed = (mine * rms * gain).astype(bf16)
    normed = normed.reshape(rows, cols // rows, CHUNKS, part, feats).transpose(0, 2, 3, 1, 4)
    normed = normed.reshape(rows, CHUNKS, part, depth)
    share = lax.all_to_all(normed, "row", 0, 0)

    flat = share.reshape(rows * CHUNKS * part, depth)
    k_part = jnp.dot(flat, w_key, preferred_element_type=f32).reshape(-1, rows, pair)
    v_part = jnp.dot(flat, w_value, preferred_element_type=f32).reshape(-1, rows, pair)

    def kv_part(d):
        return jnp.concatenate(
            [
                lax.dynamic_index_in_dim(k_part, d, 1, keepdims=False),
                lax.dynamic_index_in_dim(v_part, d, 1, keepdims=False),
            ],
            axis=1,
        )

    kv = ring_sum(kv_part, row, rows)
    tables = [
        lax.dynamic_index_in_dim(
            t.reshape(rows, CHUNKS, cols, part, HD), col, 2, keepdims=False
        ).reshape(-1, 1, HD)
        for t in (cos_all, sin_all)
    ]
    k_rot = rope(kv[:, :pair].reshape(-1, 2, HD), *tables).astype(bf16)
    v_cast = kv[:, pair:].reshape(-1, 2, HD).astype(bf16)
    both = jnp.stack([k_rot, v_cast]).transpose(2, 0, 1, 3)
    side = col // 4
    keep = lax.dynamic_index_in_dim(both, side, 0, keepdims=True)
    give = lax.dynamic_index_in_dim(both, 1 - side, 0, keepdims=True)
    for bit in (4, 2, 1):
        came = lax.ppermute(
            give if bit == 4 else keep, "col", [(i, i ^ bit) for i in range(cols)]
        )
        keep = jnp.concatenate([keep, came], axis=0)
    kv_all = jnp.zeros((2, rows, CHUNKS, cols, part, HD), bf16)
    for i, k in enumerate((0, 4, 2, 6, 1, 5, 3, 7)):
        kv_all = lax.dynamic_update_slice(
            kv_all,
            keep[i].reshape(2, rows, CHUNKS, 1, part, HD),
            (0, 0, 0, col ^ k, 0, 0),
        )
    keys = kv_all[0].reshape(total_tokens, HD)
    values = kv_all[1].reshape(total_tokens, HD)

    w_pieces = []
    for m in range(cols // 2):
        which = (col // 2 + m) % (cols // 2)
        piece = lax.dynamic_slice_in_dim(w_query, which * pair, pair, 1)
        w_pieces.append(
            lax.ppermute(
                piece,
                "col",
                [(i, 4 * (i % 2) + (i // 2 + m) % 4) for i in range(cols)],
            )
        )
    w_heads = jnp.concatenate(w_pieces, axis=1)
    w_rows = w_out.reshape(cols, pair, w_out.shape[1])
    w_turned = jnp.concatenate(
        [lax.dynamic_index_in_dim(w_rows, col ^ k, 0, keepdims=False) for k in range(cols)],
        axis=0,
    )

    outs = []
    for j in range(CHUNKS):
        pieces = plane_pieces(share[:, j].reshape(rows * part, depth), core, cols)
        whole = jnp.zeros((cols, rows * part, depth), bf16)
        for k, piece in enumerate(pieces):
            whole = lax.dynamic_update_slice(whole, piece[None], (col ^ k, 0, 0))
        q_part = jnp.dot(
            whole.reshape(cols * rows * part, depth), w_heads, preferred_element_type=f32
        ).reshape(-1, rows, pair)

        def query_part(d, q_part=q_part):
            return lax.dynamic_index_in_dim(q_part, (col % 4 - d) % rows, 1, keepdims=False)

        q_sum = ring_sum(query_part, row, rows).reshape(cols, rows, part, 2, HD)
        q_sum = q_sum.transpose(1, 3, 0, 2, 4).reshape(rows, 2, tile_rows, HD)
        q_tables = [
            t.reshape(rows, CHUNKS, 1, tile_rows, HD)[:, j] for t in (cos_all, sin_all)
        ]
        q_rot = rope(q_sum, *q_tables).astype(bf16)
        context = attend(q_rot, keys, values, doc_ends, j * tile_rows, tok_rows)
        mixed = jnp.concatenate(
            plane_pieces(context.reshape(rows * tile_rows, pair), core, cols), axis=1
        )
        o_part = jnp.dot(mixed, w_turned, preferred_element_type=f32).reshape(
            rows, tile_rows, feats
        )

        def out_part(d, o_part=o_part):
            return lax.dynamic_index_in_dim(o_part, d, 0, keepdims=False)

        outs.append(ring_sum(out_part, row, rows))
    projected = jnp.concatenate(outs, axis=0)
    return (tokens.astype(f32) + projected).astype(bf16)


def gathered_body(tokens, norm_gain, w_query, w_key, w_value, w_out, doc_lengths):
    tok_rows = tokens.shape[0]
    col_index = lax.axis_index("col")
    row_index = lax.axis_index("row")
    query_cols = w_query.shape[1]
    local_heads = query_cols // HD
    group_size = HEADS // KVH
    kv_head = col_index * local_heads // group_size
    key_cols = lax.dynamic_slice_in_dim(w_key, kv_head * HD, HD, 1)
    value_cols = lax.dynamic_slice_in_dim(w_value, kv_head * HD, HD, 1)
    gathered = lax.all_gather(tokens, "col", axis=1, tiled=True)
    whole_f = gathered.astype(jnp.float32)
    whole_rms = lax.rsqrt(jnp.mean(whole_f * whole_f, axis=1, keepdims=True) + norm_eps)
    normed = (whole_f * whole_rms * norm_gain.astype(jnp.float32)[None, :]).astype(jnp.bfloat16)
    queries = jnp.dot(
        normed,
        lax.all_gather(w_query, "row", axis=0, tiled=True),
        preferred_element_type=jnp.float32,
    )
    keys_f = jnp.dot(
        normed,
        lax.all_gather(key_cols, "row", axis=0, tiled=True),
        preferred_element_type=jnp.float32,
    )
    values_f = jnp.dot(
        normed,
        lax.all_gather(value_cols, "row", axis=0, tiled=True),
        preferred_element_type=jnp.float32,
    )
    positions = row_index * tok_rows + jnp.arange(tok_rows, dtype=jnp.int32)
    cosine, sine = rope_tables(positions, HD)
    q_rot = rotate(queries.reshape(tok_rows, local_heads, HD), cosine, sine).astype(jnp.bfloat16)
    k_rot = (
        rotate(keys_f.reshape(tok_rows, 1, HD), cosine, sine)
        .reshape(tok_rows, HD)
        .astype(jnp.bfloat16)
    )
    v_cast = values_f.astype(jnp.bfloat16)
    doc_ends = running_sums(doc_lengths)
    query_docs = doc_index(positions, doc_ends)
    score_scale = HD ** (-0.5)
    start_state = (
        jnp.full((local_heads, tok_rows), masked_value, jnp.float32),
        jnp.zeros((local_heads, tok_rows), jnp.float32),
        jnp.zeros((local_heads, tok_rows, HD), jnp.float32),
    )
    key_piece = lax.all_gather(k_rot, "row", axis=0, tiled=True)
    value_piece = lax.all_gather(v_cast, "row", axis=0, tiled=True)
    blocks = key_piece.shape[0] // tok_rows
    key_blocks = key_piece.reshape(blocks, tok_rows, HD)
    value_blocks = value_piece.reshape(blocks, tok_rows, HD)

    def visit(state, block_in):
        key_block, value_block, block_number = block_in
        run_max, run_total, run_acc = state
        key_pos = block_number * tok_rows + jnp.arange(tok_rows, dtype=jnp.int32)
        allowed = (query_docs[:, None] == doc_index(key_pos, doc_ends)[None, :]) & (
            key_pos[None, :] <= positions[:, None]
        )
        scores = (
            jnp.einsum("qhd,kd->hqk", q_rot, key_block, preferred_element_type=jnp.float32)
            * score_scale
        )
        masked = jnp.where(allowed[None], scores, masked_value)
        new_max = jnp.maximum(run_max, jnp.max(masked, axis=2))
        factor = jnp.exp(run_max - new_max)
        weights = jnp.where(allowed[None], jnp.exp(masked - new_max[:, :, None]), 0.0)
        new_total = run_total * factor + jnp.sum(weights, axis=2)
        new_acc = run_acc * factor[:, :, None] + jnp.einsum(
            "hqk,kd->hqd",
            weights.astype(jnp.bfloat16),
            value_block,
            preferred_element_type=jnp.float32,
        )
        return ((new_max, new_total, new_acc), None)

    final_state, unused = lax.scan(
        visit, start_state, (key_blocks, value_blocks, jnp.arange(blocks, dtype=jnp.int32))
    )
    run_max, run_total, run_acc = final_state
    context = (
        (run_acc / run_total[:, :, None])
        .astype(jnp.bfloat16)
        .transpose(1, 0, 2)
        .reshape(tok_rows, query_cols)
    )
    weight_whole = lax.all_gather(w_out, "row", axis=0, tiled=True)
    projected = jnp.dot(
        lax.all_gather(context, "col", axis=1, tiled=True),
        weight_whole,
        preferred_element_type=jnp.float32,
    )
    return (tokens.astype(jnp.float32) + projected).astype(jnp.bfloat16)


def solution(mesh):
    rows, cols = mesh.shape["row"], mesh.shape["col"]
    if (rows, cols) == (4, 8):
        body = functools.partial(stationary_body, rows, cols)
    else:
        body = gathered_body
    return jax.shard_map(
        body,
        mesh=mesh,
        in_specs=(
            P("row", "col"),
            P(),
            P("row", "col"),
            P("row", None),
            P("row", None),
            P("row", "col"),
            P(),
        ),
        out_specs=P("row", "col"),
        check_vma=False,
    )
```

```python
import functools

import jax
import jax.numpy as jnp
from jax import lax
from jax.experimental import pallas as pl
from jax.experimental.pallas import tpu as pltpu
from jax.sharding import PartitionSpec as P

HEADS = 64
KVH = 8
HD = 128


rope_base = 500000.0
norm_eps = 1e-05
masked_value = -1e30
f32 = jnp.float32
bf16 = jnp.bfloat16


def rope_tables(positions, head_dim):
    freq_index = jnp.arange(head_dim // 2, dtype=jnp.int32).astype(jnp.float32)
    inverse = rope_base ** (-2.0 * freq_index / head_dim)
    angles = positions.astype(jnp.float32)[:, None] * inverse[None, :]
    return (jnp.cos(angles), jnp.sin(angles))


def rotate(vectors, cosine, sine):
    half_dim = vectors.shape[-1] // 2
    first = vectors[..., :half_dim]
    second = vectors[..., half_dim:]
    cos_part = cosine[:, None, :]
    sin_part = sine[:, None, :]
    return jnp.concatenate(
        [first * cos_part - second * sin_part, second * cos_part + first * sin_part], axis=-1
    )


def running_sums(doc_lengths):
    ends, total = [], jnp.int32(0)
    for i in range(doc_lengths.shape[0]):
        total = total + doc_lengths[i]
        ends.append(total)
    return jnp.stack(ends)


def doc_index(positions, doc_ends):
    return jnp.sum((positions[:, None] >= doc_ends[None, :]).astype(jnp.int32), axis=1)


PARTS = (16, 32, 32)
STEPS = (
    1, 0, 1, 2, 0, 1, 1, 0, 2, 3, 1, 0, 2, 2, 1, 0, 3, 1, 2, 0, 3, 3, 2, 0,
    1, 3, 1, 2, 2, 3, 1, 1, 2, 1, 3, 3, 2, 2, 1, 3, 2, 3, 1, 3, 2, 3, 2, 3,
    3,
)
KEY_BLOCK = 512
VMEM = 56 * 2**20
LESS_VMEM = 24 * 2**20
COST = pl.CostEstimate(flops=1, bytes_accessed=1, transcendentals=0)


def offsets(parts):
    return [sum(parts[:j]) for j in range(len(parts))]


class Order:
    def __init__(self):
        self.last = ()

    def __call__(self, *arrays):
        tied = lax.optimization_barrier((*arrays, *self.last))
        self.last = (tied[0],)
        return tied[0] if len(arrays) == 1 else tied[: len(arrays)]


class Strand:
    def __init__(self, order, steps):
        self.order, self.steps, self.result = order, steps, None
        self.waits = next(steps)

    def step(self):
        try:
            self.waits = self.steps.send(self.order(*self.waits) if self.waits else None)
        except StopIteration as end:
            self.result = end.value


def kv_matmul(share, w_key, w_value, rows):
    tokens, depth = share.shape
    pair = 2 * HD

    def kernel(x_ref, k_ref, v_ref, o_ref):
        o_ref[0, :, :pair] = jnp.dot(x_ref[...], k_ref[...], preferred_element_type=f32)
        o_ref[0, :, pair:] = jnp.dot(x_ref[...], v_ref[...], preferred_element_type=f32)

    return pl.pallas_call(
        kernel,
        grid=(rows,),
        in_specs=[
            pl.BlockSpec((tokens, depth), lambda d: (0, 0)),
            pl.BlockSpec((depth, pair), lambda d: (0, d)),
            pl.BlockSpec((depth, pair), lambda d: (0, d)),
        ],
        out_specs=pl.BlockSpec((1, tokens, 2 * pair), lambda d: (d, 0, 0)),
        out_shape=jax.ShapeDtypeStruct((rows, tokens, 2 * pair), f32),
        compiler_params=pltpu.CompilerParams(vmem_limit_bytes=LESS_VMEM),
        cost_estimate=COST,
        name="kv_matmul",
    )(share, w_key, w_value)


def turn(vectors, cosine, sine):
    return vectors * cosine + pltpu.roll(vectors, HD // 2, 1) * sine


def kv_finish(where, came, part, cosine, sine):
    tokens = came.shape[0]
    pair = 2 * HD

    def kernel(at_ref, came_ref, part_ref, cos_ref, sin_ref, keep_ref, give_ref):
        side = at_ref[1]
        for o_ref, head in ((keep_ref, side), (give_ref, 1 - side)):
            for i in range(2):
                cut = pl.ds(pl.multiple_of(i * pair + head * HD, HD), HD)
                whole = came_ref[:, cut].astype(f32) + part_ref[0, :, cut]
                if i == 0:
                    whole = turn(whole, cos_ref[...], sin_ref[...])
                o_ref[i] = whole.astype(bf16)

    full = lambda i, at: (0, 0)
    out = pl.BlockSpec((2, tokens, HD), lambda i, at: (0, 0, 0))
    return pl.pallas_call(
        kernel,
        grid_spec=pltpu.PrefetchScalarGridSpec(
            num_scalar_prefetch=1,
            grid=(1,),
            in_specs=[
                pl.BlockSpec((tokens, 2 * pair), full),
                pl.BlockSpec((1, tokens, 2 * pair), lambda i, at: (at[0], 0, 0)),
                pl.BlockSpec((tokens, HD), full),
                pl.BlockSpec((tokens, HD), full),
            ],
            out_specs=[out, out],
        ),
        out_shape=[jax.ShapeDtypeStruct((2, tokens, HD), bf16)] * 2,
        compiler_params=pltpu.CompilerParams(vmem_limit_bytes=VMEM),
        cost_estimate=COST,
        name="kv_finish",
    )(where, came, part, cosine, sine)


def kv_assemble(col, pieces, rows, tok_rows, parts):
    cols = len(pieces)
    share = pieces[0].shape[1] // rows

    def kernel(col_ref, *refs):
        o_ref = refs[-1]
        for k in range(cols):
            source = col_ref[0] ^ k
            for t in range(rows):
                for off, size in zip(offsets(parts), parts):
                    first = t * tok_rows + off * cols
                    at = pl.multiple_of(first + source * size, 16)
                    here = t * share + off
                    for i in range(2):
                        o_ref[i, pl.ds(at, size), :] = refs[k][i, here : here + size, :]

    return pl.pallas_call(
        kernel,
        in_specs=[pl.BlockSpec(memory_space=pltpu.SMEM)]
        + [pl.BlockSpec(memory_space=pltpu.VMEM)] * cols,
        out_specs=pl.BlockSpec(memory_space=pltpu.VMEM),
        out_shape=jax.ShapeDtypeStruct((2, rows * tok_rows, HD), bf16),
        compiler_params=pltpu.CompilerParams(vmem_limit_bytes=VMEM),
        cost_estimate=COST,
        name="kv_assemble",
    )(col, *pieces)


def query_matmul(col, pieces, weights, w_query, rows, size):
    pairs = len(pieces)
    cols, depth = 2 * pairs, pieces[0].shape[2]
    group = rows * size
    pair = weights[0].shape[1]
    n = len(weights)

    def kernel(col_ref, *refs):
        x_refs, w_refs = refs[:pairs], refs[pairs : pairs + n]
        own_ref, o_ref, xs, ws, x_sem, w_sem = refs[pairs + n :]
        m = pl.program_id(0)
        col = col_ref[0]

        @pl.when(m == 0)
        def _():
            copies = []
            for i, both in enumerate(source_of(col)):
                for h, source in enumerate(both):
                    at = pl.multiple_of(source * group, group)
                    copies.append(
                        pltpu.make_async_copy(
                            x_refs[i].at[h], xs.at[pl.ds(at, group), :], x_sem.at[2 * i + h]
                        )
                    )
            for copy in copies:
                copy.start()
            for i in range(n):
                held = (col // 2 + i) % n
                stays = col == 4 * (col % 2) + held
                cut = pl.ds(pl.multiple_of(held * pair, pair), pair)

                @pl.when(stays)
                def _(i=i, cut=cut):
                    pltpu.make_async_copy(own_ref.at[:, cut], ws.at[i], w_sem.at[i]).start()

                @pl.when(jnp.logical_not(stays))
                def _(i=i):
                    pltpu.make_async_copy(w_refs[i], ws.at[i], w_sem.at[i]).start()

            for copy in copies:
                copy.wait()

        pltpu.make_async_copy(w_refs[0], ws.at[m], w_sem.at[m]).wait()

        total = jnp.dot(xs[...], ws[m], preferred_element_type=f32)
        for c in range(cols):
            for t in range(rows):
                first = (c * rows + t) * size
                o_ref[0, t, c * size : (c + 1) * size, :] = total[first : first + size, :]

    return pl.pallas_call(
        kernel,
        grid=(n,),
        in_specs=[pl.BlockSpec(memory_space=pltpu.SMEM)]
        + [pl.BlockSpec(memory_space=pl.ANY)] * (pairs + n + 1),
        out_specs=pl.BlockSpec((1, rows, cols * size, pair), lambda m: (m, 0, 0, 0)),
        out_shape=jax.ShapeDtypeStruct((n, rows, cols * size, pair), f32),
        scratch_shapes=[
            pltpu.VMEM((cols * group, depth), bf16),
            pltpu.VMEM((n, depth, pair), bf16),
            pltpu.SemaphoreType.DMA((cols,)),
            pltpu.SemaphoreType.DMA((n,)),
        ],
        compiler_params=pltpu.CompilerParams(vmem_limit_bytes=VMEM),
        cost_estimate=COST,
        name="query_matmul",
    )(col, *pieces, *weights, w_query)


def attention_kernel(first_of, tok_rows, at_ref, ends_ref, came_ref, part_ref, cos_ref, sin_ref, k_ref, v_ref, o_ref):
    docs = ends_ref.shape[0]
    size = came_ref.shape[1]
    first = pl.program_id(0) * tok_rows + first_of
    heads = []
    for h in range(2):
        cut = slice(h * HD, (h + 1) * HD)
        whole = came_ref[0, :, cut].astype(f32) + part_ref[0, 0, :, cut]
        heads.append(turn(whole, cos_ref[...], sin_ref[...]).astype(bf16))
    queries = jnp.concatenate(heads, axis=0)
    row = lax.broadcasted_iota(jnp.int32, (2 * size, 1), 0)
    pos = first + jnp.where(row >= size, row - size, row)
    start = jnp.zeros_like(pos)
    low = jnp.int32(0)
    for e in range(docs - 1):
        end = ends_ref[e]
        start = jnp.where(pos >= end, end, start)
        low = jnp.where(first >= end, end, low)
    scale = HD ** (-0.5)

    def visit(block, state):
        run_max, run_total, run_acc = state
        at = pl.multiple_of(block * KEY_BLOCK, KEY_BLOCK)
        keys = k_ref[0, pl.ds(at, KEY_BLOCK), :]
        values = v_ref[0, pl.ds(at, KEY_BLOCK), :]
        scores = lax.dot_general(
            queries, keys, (((1,), (1,)), ((), ())), preferred_element_type=f32
        )
        key_pos = at + lax.broadcasted_iota(jnp.int32, (1, KEY_BLOCK), 1)
        allowed = (key_pos <= pos) & (key_pos >= start)
        masked = jnp.where(allowed, scores, masked_value)
        new_max = jnp.maximum(run_max, jnp.max(masked, axis=1, keepdims=True))
        factor = jnp.exp((run_max - new_max) * scale)
        weights = jnp.where(allowed, jnp.exp((masked - new_max) * scale), 0.0)
        new_total = run_total * factor + jnp.sum(weights, axis=1, keepdims=True)
        new_acc = run_acc * factor + jnp.dot(
            weights.astype(bf16), values, preferred_element_type=f32
        )
        return new_max, new_total, new_acc

    state = (
        jnp.full((2 * size, 1), masked_value, f32),
        jnp.zeros((2 * size, 1), f32),
        jnp.zeros((2 * size, HD), f32),
    )
    last = (first + size - 1) // KEY_BLOCK + 1
    run_max, run_total, run_acc = lax.fori_loop(low // KEY_BLOCK, last, visit, state)
    context = (run_acc / run_total).astype(bf16)
    o_ref[0, :, :HD] = context[:size]
    o_ref[0, :, HD:] = context[size:]


def attend(which, came, part, cosine, sine, kv, doc_ends, first_of, tok_rows):
    rows, size, pair = came.shape
    total = kv.shape[1]
    table = pl.BlockSpec((size, HD), lambda g, at, ends: (g, 0))
    return pl.pallas_call(
        functools.partial(attention_kernel, first_of, tok_rows),
        grid_spec=pltpu.PrefetchScalarGridSpec(
            num_scalar_prefetch=2,
            grid=(rows,),
            in_specs=[
                pl.BlockSpec((1, size, pair), lambda g, at, ends: (g, 0, 0)),
                pl.BlockSpec((1, 1, size, pair), lambda g, at, ends: (at[0], g, 0, 0)),
                table,
                table,
                pl.BlockSpec((1, total, HD), lambda g, at, ends: (0, 0, 0)),
                pl.BlockSpec((1, total, HD), lambda g, at, ends: (1, 0, 0)),
            ],
            out_specs=pl.BlockSpec((1, size, pair), lambda g, at, ends: (g, 0, 0)),
        ),
        out_shape=jax.ShapeDtypeStruct((rows, size, pair), bf16),
        compiler_params=pltpu.CompilerParams(vmem_limit_bytes=LESS_VMEM),
        cost_estimate=COST,
        name="attend",
    )(which, doc_ends, came, part, cosine, sine, kv, kv)


def out_matmul(col, pieces, w_out, rows):
    pairs = len(pieces)
    pair = pieces[0].shape[2]
    size = pieces[0].shape[1] // rows
    depth, width = w_out.shape

    def kernel(col_ref, *refs):
        x_refs, (w_ref, o_ref, xs) = refs[:pairs], refs[pairs:]
        for i, both in enumerate(source_of(col_ref[0])):
            for h, source in enumerate(both):
                at = pl.multiple_of(source * pair, pair)
                xs[:, pl.ds(at, pair)] = x_refs[i][h]
        o_ref[0] = jnp.dot(xs[...], w_ref[...], preferred_element_type=f32)

    return pl.pallas_call(
        kernel,
        grid=(rows,),
        in_specs=[pl.BlockSpec(memory_space=pltpu.SMEM)]
        + [pl.BlockSpec((2, size, pair), lambda t: (0, t, 0))] * pairs
        + [pl.BlockSpec((depth, width), lambda t: (0, 0))],
        out_specs=pl.BlockSpec((1, size, width), lambda t: (t, 0, 0)),
        out_shape=jax.ShapeDtypeStruct((rows, size, width), f32),
        scratch_shapes=[pltpu.VMEM((size, depth), bf16)],
        compiler_params=pltpu.CompilerParams(vmem_limit_bytes=LESS_VMEM),
        cost_estimate=COST,
        name="out_matmul",
    )(col, *pieces, w_out)


def plane_gather(order, own, cols):
    def send(x, even, odd):
        return lax.ppermute(x, "col", [(i, i ^ (odd if i % 2 else even)) for i in range(cols)])

    first = yield (send(own, 2, 4),)
    two = order(jnp.stack([own, first]))
    beside = send(two, 1, 1)
    second = yield (send(two, 4, 2),)
    across, beside = yield (send(second, 1, 1), beside)
    return [two, second, beside, across]


def source_of(col):
    a = 2 + 2 * (col % 2)
    return [[col ^ k for k in ks] for ks in ((0, a), (6 - a, 6), (1, 7 - a), (a ^ 1, 7))]


def ring(order, part_of, row_index, rows):
    onward = [(i, (i + 1) % rows) for i in range(rows)]
    total = part_of((row_index - 1) % rows).astype(bf16)
    for step in range(1, rows):
        came = yield (lax.ppermute(order(total), "row", onward),)
        total = came.astype(f32) + part_of((row_index - 1 - step) % rows)
        total = total.astype(bf16)
    return came


def stationary_body(rows, cols, tokens, norm_gain, w_query, w_key, w_value, w_out, doc_lengths):
    tok_rows, feats = tokens.shape
    col = lax.axis_index("col")
    row = lax.axis_index("row")
    col_at = col[None].astype(jnp.int32)
    depth = w_query.shape[0]
    share_rows = tok_rows // cols
    parts = PARTS
    starts = offsets(parts)
    pair = 2 * HD
    doc_ends = running_sums(doc_lengths)

    order = Order()
    spread = jnp.concatenate(
        [
            tokens[a * cols : (a + p) * cols].reshape(cols, p, feats)
            for a, p in zip(starts, parts)
        ],
        axis=1,
    )
    mine = lax.all_to_all(order(spread), "col", 0, 0)

    w_pieces = []
    for m in range(cols // 2):
        which = (col // 2 + m) % (cols // 2)
        w_pieces.append(lax.dynamic_slice_in_dim(w_query, which * pair, pair, 1))
    w_pieces = list(order(*w_pieces))
    for m in range(cols // 2):
        moves = [(i, 4 * (i % 2) + (i // 2 + m) % 4) for i in range(cols)]
        moves = [(i, to) for i, to in moves if i != to]
        w_pieces[m] = lax.ppermute(w_pieces[m], "col", moves)

    positions = jnp.arange(rows * tok_rows, dtype=jnp.int32)
    cosine, sine = rope_tables(positions, HD)
    cos_all = jnp.concatenate([cosine, cosine], axis=1).reshape(rows, tok_rows, HD)
    sin_all = jnp.concatenate([-sine, sine], axis=1).reshape(rows, tok_rows, HD)

    def of_mine(table):
        return jnp.concatenate(
            [
                lax.dynamic_slice_in_dim(table, a * cols + col * p, p, 1)
                for a, p in zip(starts, parts)
            ],
            axis=1,
        ).reshape(-1, HD)

    tables = [of_mine(cos_all), of_mine(sin_all)]
    for a, p in zip(starts, parts):
        tables += [t[:, a * cols : (a + p) * cols].reshape(-1, HD) for t in (cos_all, sin_all)]
    tables = order(*tables)

    mine = order(mine).astype(f32)
    rms = lax.rsqrt(jnp.mean(mine * mine, axis=(0, 2), keepdims=True) + norm_eps)
    gain = norm_gain.astype(f32).reshape(cols, 1, feats)
    normed = (mine * rms * gain).astype(bf16)
    normed = normed.reshape(rows, cols // rows, share_rows, feats).transpose(0, 2, 1, 3)
    normed = normed.reshape(rows, share_rows, depth)
    share = lax.all_to_all(order(normed), "row", 0, 0)

    share = order(share)

    where = jnp.stack([row, col // 4]).astype(jnp.int32)
    which = ((col % 4 - row) % rows)[None].astype(jnp.int32)

    def keys_and_values():
        part = kv_matmul(share.reshape(-1, depth), w_key, w_value, rows)
        came = yield from ring(
            order, lambda d: lax.dynamic_index_in_dim(part, d, 0, keepdims=False), row, rows
        )
        keep, give = order(*kv_finish(where, came, part, tables[0], tables[1]))
        pieces = {0: keep}
        pieces[4] = yield (lax.ppermute(give, "col", [(i, i ^ 4) for i in range(cols)]),)
        for bit in (2, 1):
            together = order(jnp.stack(list(pieces.values())))
            came = yield (lax.ppermute(together, "col", [(i, i ^ bit) for i in range(cols)]),)
            for i, k in enumerate(list(pieces)):
                pieces[k ^ bit] = came[i]
        return order(
            kv_assemble(col_at, [pieces[k] for k in range(cols)], rows, tok_rows, parts)
        )

    def chunk(j):
        a, p = starts[j], parts[j]
        own = order(share[:, a : a + p].reshape(rows * p, depth))
        pieces = yield from plane_gather(order, own, cols)
        q_part = query_matmul(col_at, pieces, w_pieces, w_query, rows, p)
        came = yield from ring(
            order,
            lambda d: lax.dynamic_index_in_dim(q_part, (col % 4 - d) % rows, 0, keepdims=False),
            row,
            rows,
        )
        yield ()
        context = attend(
            which, came, q_part, *tables[2 + 2 * j : 4 + 2 * j], strands[0].result, doc_ends, a * cols, tok_rows
        )
        context = order(context.reshape(rows * p * cols, pair))
        pieces = yield from plane_gather(order, context, cols)
        o_part = out_matmul(col_at, pieces, w_out, rows)
        came = yield from ring(
            order, lambda d: lax.dynamic_index_in_dim(o_part, d, 0, keepdims=False), row, rows
        )
        own = lax.dynamic_index_in_dim(o_part, row, 0, keepdims=False)
        mine = tokens[a * cols : (a + p) * cols].astype(f32)
        return order((mine + (came.astype(f32) + own)).astype(bf16))

    strands = {}
    for n, i in enumerate(STEPS):
        if n == 2:
            w_pieces = list(order(*w_pieces))
        if i in strands:
            strands[i].step()
        else:
            strands[i] = Strand(order, chunk(i - 1) if i else keys_and_values())
    return jnp.concatenate([strands[j + 1].result for j in range(len(parts))], axis=0)


def gathered_body(tokens, norm_gain, w_query, w_key, w_value, w_out, doc_lengths):
    tok_rows = tokens.shape[0]
    col_index = lax.axis_index("col")
    row_index = lax.axis_index("row")
    query_cols = w_query.shape[1]
    local_heads = query_cols // HD
    group_size = HEADS // KVH
    kv_head = col_index * local_heads // group_size
    key_cols = lax.dynamic_slice_in_dim(w_key, kv_head * HD, HD, 1)
    value_cols = lax.dynamic_slice_in_dim(w_value, kv_head * HD, HD, 1)
    gathered = lax.all_gather(tokens, "col", axis=1, tiled=True)
    whole_f = gathered.astype(jnp.float32)
    whole_rms = lax.rsqrt(jnp.mean(whole_f * whole_f, axis=1, keepdims=True) + norm_eps)
    normed = (whole_f * whole_rms * norm_gain.astype(jnp.float32)[None, :]).astype(jnp.bfloat16)
    queries = jnp.dot(
        normed,
        lax.all_gather(w_query, "row", axis=0, tiled=True),
        preferred_element_type=jnp.float32,
    )
    keys_f = jnp.dot(
        normed,
        lax.all_gather(key_cols, "row", axis=0, tiled=True),
        preferred_element_type=jnp.float32,
    )
    values_f = jnp.dot(
        normed,
        lax.all_gather(value_cols, "row", axis=0, tiled=True),
        preferred_element_type=jnp.float32,
    )
    positions = row_index * tok_rows + jnp.arange(tok_rows, dtype=jnp.int32)
    cosine, sine = rope_tables(positions, HD)
    q_rot = rotate(queries.reshape(tok_rows, local_heads, HD), cosine, sine).astype(jnp.bfloat16)
    k_rot = (
        rotate(keys_f.reshape(tok_rows, 1, HD), cosine, sine)
        .reshape(tok_rows, HD)
        .astype(jnp.bfloat16)
    )
    v_cast = values_f.astype(jnp.bfloat16)
    doc_ends = running_sums(doc_lengths)
    query_docs = doc_index(positions, doc_ends)
    score_scale = HD ** (-0.5)
    start_state = (
        jnp.full((local_heads, tok_rows), masked_value, jnp.float32),
        jnp.zeros((local_heads, tok_rows), jnp.float32),
        jnp.zeros((local_heads, tok_rows, HD), jnp.float32),
    )
    key_piece = lax.all_gather(k_rot, "row", axis=0, tiled=True)
    value_piece = lax.all_gather(v_cast, "row", axis=0, tiled=True)
    blocks = key_piece.shape[0] // tok_rows
    key_blocks = key_piece.reshape(blocks, tok_rows, HD)
    value_blocks = value_piece.reshape(blocks, tok_rows, HD)

    def visit(state, block_in):
        key_block, value_block, block_number = block_in
        run_max, run_total, run_acc = state
        key_pos = block_number * tok_rows + jnp.arange(tok_rows, dtype=jnp.int32)
        allowed = (query_docs[:, None] == doc_index(key_pos, doc_ends)[None, :]) & (
            key_pos[None, :] <= positions[:, None]
        )
        scores = (
            jnp.einsum("qhd,kd->hqk", q_rot, key_block, preferred_element_type=jnp.float32)
            * score_scale
        )
        masked = jnp.where(allowed[None], scores, masked_value)
        new_max = jnp.maximum(run_max, jnp.max(masked, axis=2))
        factor = jnp.exp(run_max - new_max)
        weights = jnp.where(allowed[None], jnp.exp(masked - new_max[:, :, None]), 0.0)
        new_total = run_total * factor + jnp.sum(weights, axis=2)
        new_acc = run_acc * factor[:, :, None] + jnp.einsum(
            "hqk,kd->hqd",
            weights.astype(jnp.bfloat16),
            value_block,
            preferred_element_type=jnp.float32,
        )
        return ((new_max, new_total, new_acc), None)

    final_state, unused = lax.scan(
        visit, start_state, (key_blocks, value_blocks, jnp.arange(blocks, dtype=jnp.int32))
    )
    run_max, run_total, run_acc = final_state
    context = (
        (run_acc / run_total[:, :, None])
        .astype(jnp.bfloat16)
        .transpose(1, 0, 2)
        .reshape(tok_rows, query_cols)
    )
    weight_whole = lax.all_gather(w_out, "row", axis=0, tiled=True)
    projected = jnp.dot(
        lax.all_gather(context, "col", axis=1, tiled=True),
        weight_whole,
        preferred_element_type=jnp.float32,
    )
    return (tokens.astype(jnp.float32) + projected).astype(jnp.bfloat16)


def solution(mesh):
    rows, cols = mesh.shape["row"], mesh.shape["col"]
    if (rows, cols) == (4, 8):
        body = functools.partial(stationary_body, rows, cols)
    else:
        body = gathered_body
    return jax.shard_map(
        body,
        mesh=mesh,
        in_specs=(
            P("row", "col"),
            P(),
            P("row", "col"),
            P("row", None),
            P("row", None),
            P("row", "col"),
            P(),
        ),
        out_specs=P("row", "col"),
        check_vma=False,
    )
```

```python
import functools

import jax
import jax.numpy as jnp
from jax import lax
from jax.experimental import pallas as pl
from jax.experimental.pallas import tpu as pltpu
from jax.sharding import PartitionSpec as P

HEADS = 64
KVH = 8
HD = 128


rope_base = 500000.0
norm_eps = 1e-05
masked_value = -1e30
f32 = jnp.float32
bf16 = jnp.bfloat16


def rope_tables(positions, head_dim):
    freq_index = jnp.arange(head_dim // 2, dtype=jnp.int32).astype(jnp.float32)
    inverse = rope_base ** (-2.0 * freq_index / head_dim)
    angles = positions.astype(jnp.float32)[:, None] * inverse[None, :]
    return (jnp.cos(angles), jnp.sin(angles))


def rotate(vectors, cosine, sine):
    half_dim = vectors.shape[-1] // 2
    first = vectors[..., :half_dim]
    second = vectors[..., half_dim:]
    cos_part = cosine[:, None, :]
    sin_part = sine[:, None, :]
    return jnp.concatenate(
        [first * cos_part - second * sin_part, second * cos_part + first * sin_part], axis=-1
    )


def running_sums(doc_lengths):
    ends, total = [], jnp.int32(0)
    for i in range(doc_lengths.shape[0]):
        total = total + doc_lengths[i]
        ends.append(total)
    return jnp.stack(ends)


def doc_index(positions, doc_ends):
    return jnp.sum((positions[:, None] >= doc_ends[None, :]).astype(jnp.int32), axis=1)


PARTS = (16, 32, 32)
STEPS = (
    1, 0, 1, 2, 0, 1, 1, 0, 2, 3, 1, 0, 2, 2, 1, 0, 3, 1, 2, 0, 3, 3, 2, 0,
    1, 3, 1, 2, 2, 3, 1, 3, 1, 2, 3, 1, 2, 2, 1, 3, 2, 3, 1, 3, 2, 3, 2, 3,
    3,
)
KEY_BLOCK = 512
VMEM = 56 * 2**20
LESS_VMEM = 24 * 2**20
COST = pl.CostEstimate(flops=1, bytes_accessed=1, transcendentals=0)


def offsets(parts):
    return [sum(parts[:j]) for j in range(len(parts))]


class Order:
    def __init__(self):
        self.last = ()

    def __call__(self, *arrays):
        tied = lax.optimization_barrier((*arrays, *self.last))
        self.last = (tied[0],)
        return tied[0] if len(arrays) == 1 else tied[: len(arrays)]


class Strand:
    def __init__(self, order, steps):
        self.order, self.steps, self.result = order, steps, None
        self.waits = next(steps)

    def step(self):
        try:
            self.waits = self.steps.send(self.order(*self.waits) if self.waits else None)
        except StopIteration as end:
            self.result = end.value


def kv_matmul(share, w_key, w_value, rows):
    tokens, depth = share.shape
    pair = 2 * HD

    def kernel(x_ref, k_ref, v_ref, o_ref):
        o_ref[0, :, :pair] = jnp.dot(x_ref[...], k_ref[...], preferred_element_type=f32)
        o_ref[0, :, pair:] = jnp.dot(x_ref[...], v_ref[...], preferred_element_type=f32)

    return pl.pallas_call(
        kernel,
        grid=(rows,),
        in_specs=[
            pl.BlockSpec((tokens, depth), lambda d: (0, 0)),
            pl.BlockSpec((depth, pair), lambda d: (0, d)),
            pl.BlockSpec((depth, pair), lambda d: (0, d)),
        ],
        out_specs=pl.BlockSpec((1, tokens, 2 * pair), lambda d: (d, 0, 0)),
        out_shape=jax.ShapeDtypeStruct((rows, tokens, 2 * pair), f32),
        compiler_params=pltpu.CompilerParams(vmem_limit_bytes=LESS_VMEM),
        cost_estimate=COST,
        name="kv_matmul",
    )(share, w_key, w_value)


def turn(vectors, cosine, sine):
    return vectors * cosine + pltpu.roll(vectors, HD // 2, 1) * sine


def kv_finish(where, came, part, cosine, sine):
    tokens = came.shape[0]
    pair = 2 * HD

    def kernel(at_ref, came_ref, part_ref, cos_ref, sin_ref, keep_ref, give_ref):
        side = at_ref[1]
        for o_ref, head in ((keep_ref, side), (give_ref, 1 - side)):
            for i in range(2):
                cut = pl.ds(pl.multiple_of(i * pair + head * HD, HD), HD)
                whole = came_ref[:, cut].astype(f32) + part_ref[0, :, cut]
                if i == 0:
                    whole = turn(whole, cos_ref[...], sin_ref[...])
                o_ref[i] = whole.astype(bf16)

    full = lambda i, at: (0, 0)
    out = pl.BlockSpec((2, tokens, HD), lambda i, at: (0, 0, 0))
    return pl.pallas_call(
        kernel,
        grid_spec=pltpu.PrefetchScalarGridSpec(
            num_scalar_prefetch=1,
            grid=(1,),
            in_specs=[
                pl.BlockSpec((tokens, 2 * pair), full),
                pl.BlockSpec((1, tokens, 2 * pair), lambda i, at: (at[0], 0, 0)),
                pl.BlockSpec((tokens, HD), full),
                pl.BlockSpec((tokens, HD), full),
            ],
            out_specs=[out, out],
        ),
        out_shape=[jax.ShapeDtypeStruct((2, tokens, HD), bf16)] * 2,
        compiler_params=pltpu.CompilerParams(vmem_limit_bytes=VMEM),
        cost_estimate=COST,
        name="kv_finish",
    )(where, came, part, cosine, sine)


def kv_assemble(col, pieces, rows, tok_rows, parts):
    cols = len(pieces)
    share = pieces[0].shape[1] // rows

    def kernel(col_ref, *refs):
        o_ref = refs[-1]
        for k in range(cols):
            source = col_ref[0] ^ k
            for t in range(rows):
                for off, size in zip(offsets(parts), parts):
                    first = t * tok_rows + off * cols
                    at = pl.multiple_of(first + source * size, 16)
                    here = t * share + off
                    for i in range(2):
                        o_ref[i, pl.ds(at, size), :] = refs[k][i, here : here + size, :]

    return pl.pallas_call(
        kernel,
        in_specs=[pl.BlockSpec(memory_space=pltpu.SMEM)]
        + [pl.BlockSpec(memory_space=pltpu.VMEM)] * cols,
        out_specs=pl.BlockSpec(memory_space=pltpu.VMEM),
        out_shape=jax.ShapeDtypeStruct((2, rows * tok_rows, HD), bf16),
        compiler_params=pltpu.CompilerParams(vmem_limit_bytes=VMEM),
        cost_estimate=COST,
        name="kv_assemble",
    )(col, *pieces)


def query_matmul(col, pieces, weights, w_query, rows, size):
    pairs = len(pieces)
    cols, depth = 2 * pairs, pieces[0].shape[2]
    group = rows * size
    pair = weights[0].shape[1]
    n = len(weights)

    def kernel(col_ref, *refs):
        x_refs, w_refs = refs[:pairs], refs[pairs : pairs + n]
        own_ref, o_ref, xs, ws, x_sem, w_sem = refs[pairs + n :]
        m = pl.program_id(0)
        col = col_ref[0]

        @pl.when(m == 0)
        def _():
            copies = []
            for i, both in enumerate(source_of(col)):
                for h, source in enumerate(both):
                    at = pl.multiple_of(source * group, group)
                    copies.append(
                        pltpu.make_async_copy(
                            x_refs[i].at[h], xs.at[pl.ds(at, group), :], x_sem.at[2 * i + h]
                        )
                    )
            for copy in copies:
                copy.start()
            for i in range(n):
                held = (col // 2 + i) % n
                stays = col == 4 * (col % 2) + held
                cut = pl.ds(pl.multiple_of(held * pair, pair), pair)

                @pl.when(stays)
                def _(i=i, cut=cut):
                    pltpu.make_async_copy(own_ref.at[:, cut], ws.at[i], w_sem.at[i]).start()

                @pl.when(jnp.logical_not(stays))
                def _(i=i):
                    pltpu.make_async_copy(w_refs[i], ws.at[i], w_sem.at[i]).start()

            for copy in copies:
                copy.wait()

        pltpu.make_async_copy(w_refs[0], ws.at[m], w_sem.at[m]).wait()

        total = jnp.dot(xs[...], ws[m], preferred_element_type=f32)
        for c in range(cols):
            for t in range(rows):
                first = (c * rows + t) * size
                o_ref[0, t, c * size : (c + 1) * size, :] = total[first : first + size, :]

    return pl.pallas_call(
        kernel,
        grid=(n,),
        in_specs=[pl.BlockSpec(memory_space=pltpu.SMEM)]
        + [pl.BlockSpec(memory_space=pl.ANY)] * (pairs + n + 1),
        out_specs=pl.BlockSpec((1, rows, cols * size, pair), lambda m: (m, 0, 0, 0)),
        out_shape=jax.ShapeDtypeStruct((n, rows, cols * size, pair), f32),
        scratch_shapes=[
            pltpu.VMEM((cols * group, depth), bf16),
            pltpu.VMEM((n, depth, pair), bf16),
            pltpu.SemaphoreType.DMA((cols,)),
            pltpu.SemaphoreType.DMA((n,)),
        ],
        compiler_params=pltpu.CompilerParams(vmem_limit_bytes=VMEM),
        cost_estimate=COST,
        name="query_matmul",
    )(col, *pieces, *weights, w_query)


def attention_kernel(first_of, tok_rows, at_ref, ends_ref, came_ref, part_ref, cos_ref, sin_ref, k_ref, v_ref, o_ref):
    docs = ends_ref.shape[0]
    size = came_ref.shape[1]
    first = pl.program_id(0) * tok_rows + first_of
    heads = []
    for h in range(2):
        cut = slice(h * HD, (h + 1) * HD)
        whole = came_ref[0, :, cut].astype(f32) + part_ref[0, 0, :, cut]
        heads.append(turn(whole, cos_ref[...], sin_ref[...]).astype(bf16))
    queries = jnp.concatenate(heads, axis=0)
    row = lax.broadcasted_iota(jnp.int32, (2 * size, 1), 0)
    pos = first + jnp.where(row >= size, row - size, row)
    start = jnp.zeros_like(pos)
    low = jnp.int32(0)
    for e in range(docs - 1):
        end = ends_ref[e]
        start = jnp.where(pos >= end, end, start)
        low = jnp.where(first >= end, end, low)
    scale = HD ** (-0.5)

    def visit(block, state):
        run_max, run_total, run_acc = state
        at = pl.multiple_of(block * KEY_BLOCK, KEY_BLOCK)
        keys = k_ref[0, pl.ds(at, KEY_BLOCK), :]
        values = v_ref[0, pl.ds(at, KEY_BLOCK), :]
        scores = lax.dot_general(
            queries, keys, (((1,), (1,)), ((), ())), preferred_element_type=f32
        )
        key_pos = at + lax.broadcasted_iota(jnp.int32, (1, KEY_BLOCK), 1)
        allowed = (key_pos <= pos) & (key_pos >= start)
        masked = jnp.where(allowed, scores, masked_value)
        new_max = jnp.maximum(run_max, jnp.max(masked, axis=1, keepdims=True))
        factor = jnp.exp((run_max - new_max) * scale)
        weights = jnp.where(allowed, jnp.exp((masked - new_max) * scale), 0.0)
        new_total = run_total * factor + jnp.sum(weights, axis=1, keepdims=True)
        new_acc = run_acc * factor + jnp.dot(
            weights.astype(bf16), values, preferred_element_type=f32
        )
        return new_max, new_total, new_acc

    state = (
        jnp.full((2 * size, 1), masked_value, f32),
        jnp.zeros((2 * size, 1), f32),
        jnp.zeros((2 * size, HD), f32),
    )
    last = (first + size - 1) // KEY_BLOCK + 1
    run_max, run_total, run_acc = lax.fori_loop(low // KEY_BLOCK, last, visit, state)
    context = (run_acc / run_total).astype(bf16)
    o_ref[0, :, :HD] = context[:size]
    o_ref[0, :, HD:] = context[size:]


def attend(which, came, part, cosine, sine, kv, doc_ends, first_of, tok_rows):
    rows, size, pair = came.shape
    total = kv.shape[1]
    table = pl.BlockSpec((size, HD), lambda g, at, ends: (g, 0))
    return pl.pallas_call(
        functools.partial(attention_kernel, first_of, tok_rows),
        grid_spec=pltpu.PrefetchScalarGridSpec(
            num_scalar_prefetch=2,
            grid=(rows,),
            in_specs=[
                pl.BlockSpec((1, size, pair), lambda g, at, ends: (g, 0, 0)),
                pl.BlockSpec((1, 1, size, pair), lambda g, at, ends: (at[0], g, 0, 0)),
                table,
                table,
                pl.BlockSpec((1, total, HD), lambda g, at, ends: (0, 0, 0)),
                pl.BlockSpec((1, total, HD), lambda g, at, ends: (1, 0, 0)),
            ],
            out_specs=pl.BlockSpec((1, size, pair), lambda g, at, ends: (g, 0, 0)),
        ),
        out_shape=jax.ShapeDtypeStruct((rows, size, pair), bf16),
        compiler_params=pltpu.CompilerParams(vmem_limit_bytes=LESS_VMEM),
        cost_estimate=COST,
        name="attend",
    )(which, doc_ends, came, part, cosine, sine, kv, kv)


def out_matmul(col, pieces, w_out, rows):
    pairs = len(pieces)
    pair = pieces[0].shape[2]
    size = pieces[0].shape[1] // rows
    depth, width = w_out.shape

    def kernel(col_ref, *refs):
        x_refs, (w_ref, o_ref, xs) = refs[:pairs], refs[pairs:]
        for i, both in enumerate(source_of(col_ref[0])):
            for h, source in enumerate(both):
                at = pl.multiple_of(source * pair, pair)
                xs[:, pl.ds(at, pair)] = x_refs[i][h]
        o_ref[0] = jnp.dot(xs[...], w_ref[...], preferred_element_type=f32)

    return pl.pallas_call(
        kernel,
        grid=(rows,),
        in_specs=[pl.BlockSpec(memory_space=pltpu.SMEM)]
        + [pl.BlockSpec((2, size, pair), lambda t: (0, t, 0))] * pairs
        + [pl.BlockSpec((depth, width), lambda t: (0, 0))],
        out_specs=pl.BlockSpec((1, size, width), lambda t: (t, 0, 0)),
        out_shape=jax.ShapeDtypeStruct((rows, size, width), f32),
        scratch_shapes=[pltpu.VMEM((size, depth), bf16)],
        compiler_params=pltpu.CompilerParams(vmem_limit_bytes=LESS_VMEM),
        cost_estimate=COST,
        name="out_matmul",
    )(col, *pieces, w_out)


def plane_gather(order, own, cols):
    def send(x, even, odd):
        return lax.ppermute(x, "col", [(i, i ^ (odd if i % 2 else even)) for i in range(cols)])

    first = yield (send(own, 2, 4),)
    two = order(jnp.stack([own, first]))
    beside = send(two, 1, 1)
    second = yield (send(two, 4, 2),)
    across, beside = yield (send(second, 1, 1), beside)
    return [two, second, beside, across]


def source_of(col):
    a = 2 + 2 * (col % 2)
    return [[col ^ k for k in ks] for ks in ((0, a), (6 - a, 6), (1, 7 - a), (a ^ 1, 7))]


def ring(order, part_of, row_index, rows):
    onward = [(i, (i + 1) % rows) for i in range(rows)]
    total = part_of((row_index - 1) % rows).astype(bf16)
    for step in range(1, rows):
        came = yield (lax.ppermute(order(total), "row", onward),)
        total = came.astype(f32) + part_of((row_index - 1 - step) % rows)
        total = total.astype(bf16)
    return came


def stationary_body(rows, cols, tokens, norm_gain, w_query, w_key, w_value, w_out, doc_lengths):
    tok_rows, feats = tokens.shape
    col = lax.axis_index("col")
    row = lax.axis_index("row")
    col_at = col[None].astype(jnp.int32)
    depth = w_query.shape[0]
    share_rows = tok_rows // cols
    parts = PARTS
    starts = offsets(parts)
    pair = 2 * HD
    doc_ends = running_sums(doc_lengths)

    order = Order()
    spread = jnp.concatenate(
        [
            tokens[a * cols : (a + p) * cols].reshape(cols, p, feats)
            for a, p in zip(starts, parts)
        ],
        axis=1,
    )
    mine = lax.all_to_all(order(spread), "col", 0, 0)

    w_pieces = []
    for m in range(cols // 2):
        which = (col // 2 + m) % (cols // 2)
        w_pieces.append(lax.dynamic_slice_in_dim(w_query, which * pair, pair, 1))
    w_pieces = list(order(*w_pieces))
    for m in range(cols // 2):
        moves = [(i, 4 * (i % 2) + (i // 2 + m) % 4) for i in range(cols)]
        moves = [(i, to) for i, to in moves if i != to]
        w_pieces[m] = lax.ppermute(w_pieces[m], "col", moves)

    positions = jnp.arange(rows * tok_rows, dtype=jnp.int32)
    cosine, sine = rope_tables(positions, HD)
    cos_all = jnp.concatenate([cosine, cosine], axis=1).reshape(rows, tok_rows, HD)
    sin_all = jnp.concatenate([-sine, sine], axis=1).reshape(rows, tok_rows, HD)

    def of_mine(table):
        return jnp.concatenate(
            [
                lax.dynamic_slice_in_dim(table, a * cols + col * p, p, 1)
                for a, p in zip(starts, parts)
            ],
            axis=1,
        ).reshape(-1, HD)

    tables = [of_mine(cos_all), of_mine(sin_all)]
    for a, p in zip(starts, parts):
        tables += [t[:, a * cols : (a + p) * cols].reshape(-1, HD) for t in (cos_all, sin_all)]
    tables = order(*tables)

    mine = order(mine).astype(f32)
    rms = lax.rsqrt(jnp.mean(mine * mine, axis=(0, 2), keepdims=True) + norm_eps)
    gain = norm_gain.astype(f32).reshape(cols, 1, feats)
    normed = (mine * rms * gain).astype(bf16)
    normed = normed.reshape(rows, cols // rows, share_rows, feats).transpose(0, 2, 1, 3)
    normed = normed.reshape(rows, share_rows, depth)
    share = lax.all_to_all(order(normed), "row", 0, 0)

    share = order(share)

    where = jnp.stack([row, col // 4]).astype(jnp.int32)
    which = ((col % 4 - row) % rows)[None].astype(jnp.int32)

    def keys_and_values():
        part = kv_matmul(share.reshape(-1, depth), w_key, w_value, rows)
        came = yield from ring(
            order, lambda d: lax.dynamic_index_in_dim(part, d, 0, keepdims=False), row, rows
        )
        keep, give = order(*kv_finish(where, came, part, tables[0], tables[1]))
        pieces = {0: keep}
        pieces[4] = yield (lax.ppermute(give, "col", [(i, i ^ 4) for i in range(cols)]),)
        for bit in (2, 1):
            together = order(jnp.stack(list(pieces.values())))
            came = yield (lax.ppermute(together, "col", [(i, i ^ bit) for i in range(cols)]),)
            for i, k in enumerate(list(pieces)):
                pieces[k ^ bit] = came[i]
        return order(
            kv_assemble(col_at, [pieces[k] for k in range(cols)], rows, tok_rows, parts)
        )

    def chunk(j):
        a, p = starts[j], parts[j]
        own = order(share[:, a : a + p].reshape(rows * p, depth))
        pieces = yield from plane_gather(order, own, cols)
        q_part = query_matmul(col_at, pieces, w_pieces, w_query, rows, p)
        came = yield from ring(
            order,
            lambda d: lax.dynamic_index_in_dim(q_part, (col % 4 - d) % rows, 0, keepdims=False),
            row,
            rows,
        )
        yield ()
        context = attend(
            which, came, q_part, *tables[2 + 2 * j : 4 + 2 * j], strands[0].result, doc_ends, a * cols, tok_rows
        )
        context = order(context.reshape(rows * p * cols, pair))
        pieces = yield from plane_gather(order, context, cols)
        o_part = out_matmul(col_at, pieces, w_out, rows)
        came = yield from ring(
            order, lambda d: lax.dynamic_index_in_dim(o_part, d, 0, keepdims=False), row, rows
        )
        own = lax.dynamic_index_in_dim(o_part, row, 0, keepdims=False)
        mine = tokens[a * cols : (a + p) * cols].astype(f32)
        return order((mine + (came.astype(f32) + own)).astype(bf16))

    strands = {}
    for n, i in enumerate(STEPS):
        if n == 2:
            w_pieces = list(order(*w_pieces))
        if i in strands:
            strands[i].step()
        else:
            strands[i] = Strand(order, chunk(i - 1) if i else keys_and_values())
    return jnp.concatenate([strands[j + 1].result for j in range(len(parts))], axis=0)


def gathered_body(tokens, norm_gain, w_query, w_key, w_value, w_out, doc_lengths):
    tok_rows = tokens.shape[0]
    col_index = lax.axis_index("col")
    row_index = lax.axis_index("row")
    query_cols = w_query.shape[1]
    local_heads = query_cols // HD
    group_size = HEADS // KVH
    kv_head = col_index * local_heads // group_size
    key_cols = lax.dynamic_slice_in_dim(w_key, kv_head * HD, HD, 1)
    value_cols = lax.dynamic_slice_in_dim(w_value, kv_head * HD, HD, 1)
    gathered = lax.all_gather(tokens, "col", axis=1, tiled=True)
    whole_f = gathered.astype(jnp.float32)
    whole_rms = lax.rsqrt(jnp.mean(whole_f * whole_f, axis=1, keepdims=True) + norm_eps)
    normed = (whole_f * whole_rms * norm_gain.astype(jnp.float32)[None, :]).astype(jnp.bfloat16)
    queries = jnp.dot(
        normed,
        lax.all_gather(w_query, "row", axis=0, tiled=True),
        preferred_element_type=jnp.float32,
    )
    keys_f = jnp.dot(
        normed,
        lax.all_gather(key_cols, "row", axis=0, tiled=True),
        preferred_element_type=jnp.float32,
    )
    values_f = jnp.dot(
        normed,
        lax.all_gather(value_cols, "row", axis=0, tiled=True),
        preferred_element_type=jnp.float32,
    )
    positions = row_index * tok_rows + jnp.arange(tok_rows, dtype=jnp.int32)
    cosine, sine = rope_tables(positions, HD)
    q_rot = rotate(queries.reshape(tok_rows, local_heads, HD), cosine, sine).astype(jnp.bfloat16)
    k_rot = (
        rotate(keys_f.reshape(tok_rows, 1, HD), cosine, sine)
        .reshape(tok_rows, HD)
        .astype(jnp.bfloat16)
    )
    v_cast = values_f.astype(jnp.bfloat16)
    doc_ends = running_sums(doc_lengths)
    query_docs = doc_index(positions, doc_ends)
    score_scale = HD ** (-0.5)
    start_state = (
        jnp.full((local_heads, tok_rows), masked_value, jnp.float32),
        jnp.zeros((local_heads, tok_rows), jnp.float32),
        jnp.zeros((local_heads, tok_rows, HD), jnp.float32),
    )
    key_piece = lax.all_gather(k_rot, "row", axis=0, tiled=True)
    value_piece = lax.all_gather(v_cast, "row", axis=0, tiled=True)
    blocks = key_piece.shape[0] // tok_rows
    key_blocks = key_piece.reshape(blocks, tok_rows, HD)
    value_blocks = value_piece.reshape(blocks, tok_rows, HD)

    def visit(state, block_in):
        key_block, value_block, block_number = block_in
        run_max, run_total, run_acc = state
        key_pos = block_number * tok_rows + jnp.arange(tok_rows, dtype=jnp.int32)
        allowed = (query_docs[:, None] == doc_index(key_pos, doc_ends)[None, :]) & (
            key_pos[None, :] <= positions[:, None]
        )
        scores = (
            jnp.einsum("qhd,kd->hqk", q_rot, key_block, preferred_element_type=jnp.float32)
            * score_scale
        )
        masked = jnp.where(allowed[None], scores, masked_value)
        new_max = jnp.maximum(run_max, jnp.max(masked, axis=2))
        factor = jnp.exp(run_max - new_max)
        weights = jnp.where(allowed[None], jnp.exp(masked - new_max[:, :, None]), 0.0)
        new_total = run_total * factor + jnp.sum(weights, axis=2)
        new_acc = run_acc * factor[:, :, None] + jnp.einsum(
            "hqk,kd->hqd",
            weights.astype(jnp.bfloat16),
            value_block,
            preferred_element_type=jnp.float32,
        )
        return ((new_max, new_total, new_acc), None)

    final_state, unused = lax.scan(
        visit, start_state, (key_blocks, value_blocks, jnp.arange(blocks, dtype=jnp.int32))
    )
    run_max, run_total, run_acc = final_state
    context = (
        (run_acc / run_total[:, :, None])
        .astype(jnp.bfloat16)
        .transpose(1, 0, 2)
        .reshape(tok_rows, query_cols)
    )
    weight_whole = lax.all_gather(w_out, "row", axis=0, tiled=True)
    projected = jnp.dot(
        lax.all_gather(context, "col", axis=1, tiled=True),
        weight_whole,
        preferred_element_type=jnp.float32,
    )
    return (tokens.astype(jnp.float32) + projected).astype(jnp.bfloat16)


def solution(mesh):
    rows, cols = mesh.shape["row"], mesh.shape["col"]
    if (rows, cols) == (4, 8):
        body = functools.partial(stationary_body, rows, cols)
    else:
        body = gathered_body
    return jax.shard_map(
        body,
        mesh=mesh,
        in_specs=(
            P("row", "col"),
            P(),
            P("row", "col"),
            P("row", None),
            P("row", None),
            P("row", "col"),
            P(),
        ),
        out_specs=P("row", "col"),
        check_vma=False,
    )
```

```python
import functools

import jax
import jax.numpy as jnp
from jax import lax
from jax.experimental import pallas as pl
from jax.experimental.pallas import tpu as pltpu
from jax.sharding import PartitionSpec as P

HEADS = 64
KVH = 8
HD = 128


rope_base = 500000.0
norm_eps = 1e-05
masked_value = -1e30
f32 = jnp.float32
bf16 = jnp.bfloat16


def rope_tables(positions, head_dim):
    freq_index = jnp.arange(head_dim // 2, dtype=jnp.int32).astype(jnp.float32)
    inverse = rope_base ** (-2.0 * freq_index / head_dim)
    angles = positions.astype(jnp.float32)[:, None] * inverse[None, :]
    return (jnp.cos(angles), jnp.sin(angles))


def rotate(vectors, cosine, sine):
    half_dim = vectors.shape[-1] // 2
    first = vectors[..., :half_dim]
    second = vectors[..., half_dim:]
    cos_part = cosine[:, None, :]
    sin_part = sine[:, None, :]
    return jnp.concatenate(
        [first * cos_part - second * sin_part, second * cos_part + first * sin_part], axis=-1
    )


def running_sums(doc_lengths):
    ends, total = [], jnp.int32(0)
    for i in range(doc_lengths.shape[0]):
        total = total + doc_lengths[i]
        ends.append(total)
    return jnp.stack(ends)


def doc_index(positions, doc_ends):
    return jnp.sum((positions[:, None] >= doc_ends[None, :]).astype(jnp.int32), axis=1)


PARTS = (16, 32, 32)
STEPS = (
    1, 2, 0, 1, 2, 0, 3, 1, 1, 0, 2, 0, 1, 2, 0, 1, 3, 2, 1, 0, 3, 3, 2, 0,
    1, 3, 1, 2, 2, 3, 1, 2, 1, 3, 1, 3, 2, 2, 1, 3, 2, 3, 1, 3, 2, 3, 3, 2,
    3,
)
KEY_BLOCK = 512
VMEM = 56 * 2**20
LESS_VMEM = 24 * 2**20
COST = pl.CostEstimate(flops=1, bytes_accessed=1, transcendentals=0)


def offsets(parts):
    return [sum(parts[:j]) for j in range(len(parts))]


class Order:
    def __init__(self):
        self.last = ()

    def __call__(self, *arrays):
        tied = lax.optimization_barrier((*arrays, *self.last))
        self.last = (tied[0],)
        return tied[0] if len(arrays) == 1 else tied[: len(arrays)]


class Strand:
    def __init__(self, order, steps):
        self.order, self.steps, self.result = order, steps, None
        self.waits = next(steps)

    def step(self):
        try:
            self.waits = self.steps.send(self.order(*self.waits) if self.waits else None)
        except StopIteration as end:
            self.result = end.value


def kv_matmul(share, w_key, w_value, rows):
    tokens, depth = share.shape
    pair = 2 * HD

    def kernel(x_ref, k_ref, v_ref, o_ref):
        o_ref[0, :, :pair] = jnp.dot(x_ref[...], k_ref[...], preferred_element_type=f32)
        o_ref[0, :, pair:] = jnp.dot(x_ref[...], v_ref[...], preferred_element_type=f32)

    return pl.pallas_call(
        kernel,
        grid=(rows,),
        in_specs=[
            pl.BlockSpec((tokens, depth), lambda d: (0, 0)),
            pl.BlockSpec((depth, pair), lambda d: (0, d)),
            pl.BlockSpec((depth, pair), lambda d: (0, d)),
        ],
        out_specs=pl.BlockSpec((1, tokens, 2 * pair), lambda d: (d, 0, 0)),
        out_shape=jax.ShapeDtypeStruct((rows, tokens, 2 * pair), f32),
        compiler_params=pltpu.CompilerParams(vmem_limit_bytes=LESS_VMEM),
        cost_estimate=COST,
        name="kv_matmul",
    )(share, w_key, w_value)


def turn(vectors, cosine, sine):
    return vectors * cosine + pltpu.roll(vectors, HD // 2, 1) * sine


def kv_finish(where, came, part, cosine, sine):
    tokens = came.shape[0]
    pair = 2 * HD

    def kernel(at_ref, came_ref, part_ref, cos_ref, sin_ref, keep_ref, give_ref):
        side = at_ref[1]
        for o_ref, head in ((keep_ref, side), (give_ref, 1 - side)):
            for i in range(2):
                cut = pl.ds(pl.multiple_of(i * pair + head * HD, HD), HD)
                whole = came_ref[:, cut].astype(f32) + part_ref[0, :, cut]
                if i == 0:
                    whole = turn(whole, cos_ref[...], sin_ref[...])
                o_ref[i] = whole.astype(bf16)

    full = lambda i, at: (0, 0)
    out = pl.BlockSpec((2, tokens, HD), lambda i, at: (0, 0, 0))
    return pl.pallas_call(
        kernel,
        grid_spec=pltpu.PrefetchScalarGridSpec(
            num_scalar_prefetch=1,
            grid=(1,),
            in_specs=[
                pl.BlockSpec((tokens, 2 * pair), full),
                pl.BlockSpec((1, tokens, 2 * pair), lambda i, at: (at[0], 0, 0)),
                pl.BlockSpec((tokens, HD), full),
                pl.BlockSpec((tokens, HD), full),
            ],
            out_specs=[out, out],
        ),
        out_shape=[jax.ShapeDtypeStruct((2, tokens, HD), bf16)] * 2,
        compiler_params=pltpu.CompilerParams(vmem_limit_bytes=VMEM),
        cost_estimate=COST,
        name="kv_finish",
    )(where, came, part, cosine, sine)


def kv_assemble(col, pieces, rows, tok_rows, parts):
    cols = len(pieces)
    share = pieces[0].shape[1] // rows

    def kernel(col_ref, *refs):
        o_ref = refs[-1]
        for k in range(cols):
            source = col_ref[0] ^ k
            for t in range(rows):
                for off, size in zip(offsets(parts), parts):
                    first = t * tok_rows + off * cols
                    at = pl.multiple_of(first + source * size, 16)
                    here = t * share + off
                    for i in range(2):
                        o_ref[i, pl.ds(at, size), :] = refs[k][i, here : here + size, :]

    return pl.pallas_call(
        kernel,
        in_specs=[pl.BlockSpec(memory_space=pltpu.SMEM)]
        + [pl.BlockSpec(memory_space=pltpu.VMEM)] * cols,
        out_specs=pl.BlockSpec(memory_space=pltpu.VMEM),
        out_shape=jax.ShapeDtypeStruct((2, rows * tok_rows, HD), bf16),
        compiler_params=pltpu.CompilerParams(vmem_limit_bytes=VMEM),
        cost_estimate=COST,
        name="kv_assemble",
    )(col, *pieces)


def query_matmul(col, pieces, weights, w_query, rows, size):
    pairs = len(pieces)
    cols, depth = 2 * pairs, pieces[0].shape[2]
    group = rows * size
    pair = weights[0].shape[1]
    n = len(weights)

    def kernel(col_ref, *refs):
        x_refs, w_refs = refs[:pairs], refs[pairs : pairs + n]
        own_ref, o_ref, xs, ws, x_sem, w_sem = refs[pairs + n :]
        m = pl.program_id(0)
        col = col_ref[0]

        @pl.when(m == 0)
        def _():
            copies = []
            for i, both in enumerate(source_of(col)):
                for h, source in enumerate(both):
                    at = pl.multiple_of(source * group, group)
                    copies.append(
                        pltpu.make_async_copy(
                            x_refs[i].at[h], xs.at[pl.ds(at, group), :], x_sem.at[2 * i + h]
                        )
                    )
            for copy in copies:
                copy.start()
            for i in range(n):
                held = (col // 2 + i) % n
                stays = col == 4 * (col % 2) + held
                cut = pl.ds(pl.multiple_of(held * pair, pair), pair)

                @pl.when(stays)
                def _(i=i, cut=cut):
                    pltpu.make_async_copy(own_ref.at[:, cut], ws.at[i], w_sem.at[i]).start()

                @pl.when(jnp.logical_not(stays))
                def _(i=i):
                    pltpu.make_async_copy(w_refs[i], ws.at[i], w_sem.at[i]).start()

            for copy in copies:
                copy.wait()

        pltpu.make_async_copy(w_refs[0], ws.at[m], w_sem.at[m]).wait()

        total = jnp.dot(xs[...], ws[m], preferred_element_type=f32)
        for c in range(cols):
            for t in range(rows):
                first = (c * rows + t) * size
                o_ref[0, t, c * size : (c + 1) * size, :] = total[first : first + size, :]

    return pl.pallas_call(
        kernel,
        grid=(n,),
        in_specs=[pl.BlockSpec(memory_space=pltpu.SMEM)]
        + [pl.BlockSpec(memory_space=pl.ANY)] * (pairs + n + 1),
        out_specs=pl.BlockSpec((1, rows, cols * size, pair), lambda m: (m, 0, 0, 0)),
        out_shape=jax.ShapeDtypeStruct((n, rows, cols * size, pair), f32),
        scratch_shapes=[
            pltpu.VMEM((cols * group, depth), bf16),
            pltpu.VMEM((n, depth, pair), bf16),
            pltpu.SemaphoreType.DMA((cols,)),
            pltpu.SemaphoreType.DMA((n,)),
        ],
        compiler_params=pltpu.CompilerParams(vmem_limit_bytes=VMEM),
        cost_estimate=COST,
        name="query_matmul",
    )(col, *pieces, *weights, w_query)


def attention_kernel(first_of, tok_rows, at_ref, ends_ref, came_ref, part_ref, cos_ref, sin_ref, k_ref, v_ref, o_ref):
    docs = ends_ref.shape[0]
    size = came_ref.shape[1]
    first = pl.program_id(0) * tok_rows + first_of
    heads = []
    for h in range(2):
        cut = slice(h * HD, (h + 1) * HD)
        whole = came_ref[0, :, cut].astype(f32) + part_ref[0, 0, :, cut]
        heads.append(turn(whole, cos_ref[...], sin_ref[...]).astype(bf16))
    queries = jnp.concatenate(heads, axis=0)
    row = lax.broadcasted_iota(jnp.int32, (2 * size, 1), 0)
    pos = first + jnp.where(row >= size, row - size, row)
    start = jnp.zeros_like(pos)
    low = jnp.int32(0)
    for e in range(docs - 1):
        end = ends_ref[e]
        start = jnp.where(pos >= end, end, start)
        low = jnp.where(first >= end, end, low)
    scale = HD ** (-0.5)

    def visit(block, state):
        run_max, run_total, run_acc = state
        at = pl.multiple_of(block * KEY_BLOCK, KEY_BLOCK)
        keys = k_ref[0, pl.ds(at, KEY_BLOCK), :]
        values = v_ref[0, pl.ds(at, KEY_BLOCK), :]
        scores = lax.dot_general(
            queries, keys, (((1,), (1,)), ((), ())), preferred_element_type=f32
        )
        key_pos = at + lax.broadcasted_iota(jnp.int32, (1, KEY_BLOCK), 1)
        allowed = (key_pos <= pos) & (key_pos >= start)
        masked = jnp.where(allowed, scores, masked_value)
        new_max = jnp.maximum(run_max, jnp.max(masked, axis=1, keepdims=True))
        factor = jnp.exp((run_max - new_max) * scale)
        weights = jnp.where(allowed, jnp.exp((masked - new_max) * scale), 0.0)
        new_total = run_total * factor + jnp.sum(weights, axis=1, keepdims=True)
        new_acc = run_acc * factor + jnp.dot(
            weights.astype(bf16), values, preferred_element_type=f32
        )
        return new_max, new_total, new_acc

    state = (
        jnp.full((2 * size, 1), masked_value, f32),
        jnp.zeros((2 * size, 1), f32),
        jnp.zeros((2 * size, HD), f32),
    )
    last = (first + size - 1) // KEY_BLOCK + 1
    run_max, run_total, run_acc = lax.fori_loop(low // KEY_BLOCK, last, visit, state)
    context = (run_acc / run_total).astype(bf16)
    o_ref[0, :, :HD] = context[:size]
    o_ref[0, :, HD:] = context[size:]


def attend(which, came, part, cosine, sine, kv, doc_ends, first_of, tok_rows):
    rows, size, pair = came.shape
    total = kv.shape[1]
    table = pl.BlockSpec((size, HD), lambda g, at, ends: (g, 0))
    return pl.pallas_call(
        functools.partial(attention_kernel, first_of, tok_rows),
        grid_spec=pltpu.PrefetchScalarGridSpec(
            num_scalar_prefetch=2,
            grid=(rows,),
            in_specs=[
                pl.BlockSpec((1, size, pair), lambda g, at, ends: (g, 0, 0)),
                pl.BlockSpec((1, 1, size, pair), lambda g, at, ends: (at[0], g, 0, 0)),
                table,
                table,
                pl.BlockSpec((1, total, HD), lambda g, at, ends: (0, 0, 0)),
                pl.BlockSpec((1, total, HD), lambda g, at, ends: (1, 0, 0)),
            ],
            out_specs=pl.BlockSpec((1, size, pair), lambda g, at, ends: (g, 0, 0)),
        ),
        out_shape=jax.ShapeDtypeStruct((rows, size, pair), bf16),
        compiler_params=pltpu.CompilerParams(vmem_limit_bytes=LESS_VMEM),
        cost_estimate=COST,
        name="attend",
    )(which, doc_ends, came, part, cosine, sine, kv, kv)


def out_matmul(col, pieces, w_out, rows):
    pairs = len(pieces)
    pair = pieces[0].shape[2]
    size = pieces[0].shape[1] // rows
    depth, width = w_out.shape

    def kernel(col_ref, *refs):
        x_refs, (w_ref, o_ref, xs) = refs[:pairs], refs[pairs:]
        for i, both in enumerate(source_of(col_ref[0])):
            for h, source in enumerate(both):
                at = pl.multiple_of(source * pair, pair)
                xs[:, pl.ds(at, pair)] = x_refs[i][h]
        o_ref[0] = jnp.dot(xs[...], w_ref[...], preferred_element_type=f32)

    return pl.pallas_call(
        kernel,
        grid=(rows,),
        in_specs=[pl.BlockSpec(memory_space=pltpu.SMEM)]
        + [pl.BlockSpec((2, size, pair), lambda t: (0, t, 0))] * pairs
        + [pl.BlockSpec((depth, width), lambda t: (0, 0))],
        out_specs=pl.BlockSpec((1, size, width), lambda t: (t, 0, 0)),
        out_shape=jax.ShapeDtypeStruct((rows, size, width), f32),
        scratch_shapes=[pltpu.VMEM((size, depth), bf16)],
        compiler_params=pltpu.CompilerParams(vmem_limit_bytes=LESS_VMEM),
        cost_estimate=COST,
        name="out_matmul",
    )(col, *pieces, w_out)


def plane_gather(order, own, cols):
    def send(x, even, odd):
        return lax.ppermute(x, "col", [(i, i ^ (odd if i % 2 else even)) for i in range(cols)])

    first = yield (send(own, 2, 4),)
    two = order(jnp.stack([own, first]))
    beside = send(two, 1, 1)
    second = yield (send(two, 4, 2),)
    across, beside = yield (send(second, 1, 1), beside)
    return [two, second, beside, across]


def source_of(col):
    a = 2 + 2 * (col % 2)
    return [[col ^ k for k in ks] for ks in ((0, a), (6 - a, 6), (1, 7 - a), (a ^ 1, 7))]


def ring(order, part_of, row_index, rows):
    onward = [(i, (i + 1) % rows) for i in range(rows)]
    total = part_of((row_index - 1) % rows).astype(bf16)
    for step in range(1, rows):
        came = yield (lax.ppermute(order(total), "row", onward),)
        total = came.astype(f32) + part_of((row_index - 1 - step) % rows)
        total = total.astype(bf16)
    return came


def stationary_body(rows, cols, tokens, norm_gain, w_query, w_key, w_value, w_out, doc_lengths):
    tok_rows, feats = tokens.shape
    col = lax.axis_index("col")
    row = lax.axis_index("row")
    col_at = col[None].astype(jnp.int32)
    depth = w_query.shape[0]
    share_rows = tok_rows // cols
    parts = PARTS
    starts = offsets(parts)
    pair = 2 * HD
    doc_ends = running_sums(doc_lengths)

    order = Order()
    spread = jnp.concatenate(
        [
            tokens[a * cols : (a + p) * cols].reshape(cols, p, feats)
            for a, p in zip(starts, parts)
        ],
        axis=1,
    )
    mine = lax.all_to_all(order(spread), "col", 0, 0)

    w_pieces = []
    for m in range(cols // 2):
        which = (col // 2 + m) % (cols // 2)
        w_pieces.append(lax.dynamic_slice_in_dim(w_query, which * pair, pair, 1))
    w_pieces = list(order(*w_pieces))
    for m in range(cols // 2):
        moves = [(i, 4 * (i % 2) + (i // 2 + m) % 4) for i in range(cols)]
        moves = [(i, to) for i, to in moves if i != to]
        w_pieces[m] = lax.ppermute(w_pieces[m], "col", moves)

    positions = jnp.arange(rows * tok_rows, dtype=jnp.int32)
    cosine, sine = rope_tables(positions, HD)
    cos_all = jnp.concatenate([cosine, cosine], axis=1).reshape(rows, tok_rows, HD)
    sin_all = jnp.concatenate([-sine, sine], axis=1).reshape(rows, tok_rows, HD)

    def of_mine(table):
        return jnp.concatenate(
            [
                lax.dynamic_slice_in_dim(table, a * cols + col * p, p, 1)
                for a, p in zip(starts, parts)
            ],
            axis=1,
        ).reshape(-1, HD)

    tables = [of_mine(cos_all), of_mine(sin_all)]
    for a, p in zip(starts, parts):
        tables += [t[:, a * cols : (a + p) * cols].reshape(-1, HD) for t in (cos_all, sin_all)]
    tables = order(*tables)

    mine = order(mine).astype(f32)
    rms = lax.rsqrt(jnp.mean(mine * mine, axis=(0, 2), keepdims=True) + norm_eps)
    gain = norm_gain.astype(f32).reshape(cols, 1, feats)
    normed = (mine * rms * gain).astype(bf16)
    normed = normed.reshape(rows, cols // rows, share_rows, feats).transpose(0, 2, 1, 3)
    normed = normed.reshape(rows, share_rows, depth)
    share = lax.all_to_all(order(normed), "row", 0, 0)

    share = order(share)

    where = jnp.stack([row, col // 4]).astype(jnp.int32)
    which = ((col % 4 - row) % rows)[None].astype(jnp.int32)

    def keys_and_values():
        part = kv_matmul(share.reshape(-1, depth), w_key, w_value, rows)
        came = yield from ring(
            order, lambda d: lax.dynamic_index_in_dim(part, d, 0, keepdims=False), row, rows
        )
        keep, give = order(*kv_finish(where, came, part, tables[0], tables[1]))
        pieces = {0: keep}
        pieces[4] = yield (lax.ppermute(give, "col", [(i, i ^ 4) for i in range(cols)]),)
        for bit in (2, 1):
            together = order(jnp.stack(list(pieces.values())))
            came = yield (lax.ppermute(together, "col", [(i, i ^ bit) for i in range(cols)]),)
            for i, k in enumerate(list(pieces)):
                pieces[k ^ bit] = came[i]
        return order(
            kv_assemble(col_at, [pieces[k] for k in range(cols)], rows, tok_rows, parts)
        )

    def chunk(j):
        a, p = starts[j], parts[j]
        own = order(share[:, a : a + p].reshape(rows * p, depth))
        pieces = yield from plane_gather(order, own, cols)
        q_part = query_matmul(col_at, pieces, w_pieces, w_query, rows, p)
        came = yield from ring(
            order,
            lambda d: lax.dynamic_index_in_dim(q_part, (col % 4 - d) % rows, 0, keepdims=False),
            row,
            rows,
        )
        yield ()
        context = attend(
            which, came, q_part, *tables[2 + 2 * j : 4 + 2 * j], strands[0].result, doc_ends, a * cols, tok_rows
        )
        context = order(context.reshape(rows * p * cols, pair))
        pieces = yield from plane_gather(order, context, cols)
        o_part = out_matmul(col_at, pieces, w_out, rows)
        came = yield from ring(
            order, lambda d: lax.dynamic_index_in_dim(o_part, d, 0, keepdims=False), row, rows
        )
        own = lax.dynamic_index_in_dim(o_part, row, 0, keepdims=False)
        mine = tokens[a * cols : (a + p) * cols].astype(f32)
        return order((mine + (came.astype(f32) + own)).astype(bf16))

    strands = {}
    for n, i in enumerate(STEPS):
        if n == 2:
            w_pieces = list(order(*w_pieces))
        if i in strands:
            strands[i].step()
        else:
            strands[i] = Strand(order, chunk(i - 1) if i else keys_and_values())
    return jnp.concatenate([strands[j + 1].result for j in range(len(parts))], axis=0)


def gathered_body(tokens, norm_gain, w_query, w_key, w_value, w_out, doc_lengths):
    tok_rows = tokens.shape[0]
    col_index = lax.axis_index("col")
    row_index = lax.axis_index("row")
    query_cols = w_query.shape[1]
    local_heads = query_cols // HD
    group_size = HEADS // KVH
    kv_head = col_index * local_heads // group_size
    key_cols = lax.dynamic_slice_in_dim(w_key, kv_head * HD, HD, 1)
    value_cols = lax.dynamic_slice_in_dim(w_value, kv_head * HD, HD, 1)
    gathered = lax.all_gather(tokens, "col", axis=1, tiled=True)
    whole_f = gathered.astype(jnp.float32)
    whole_rms = lax.rsqrt(jnp.mean(whole_f * whole_f, axis=1, keepdims=True) + norm_eps)
    normed = (whole_f * whole_rms * norm_gain.astype(jnp.float32)[None, :]).astype(jnp.bfloat16)
    queries = jnp.dot(
        normed,
        lax.all_gather(w_query, "row", axis=0, tiled=True),
        preferred_element_type=jnp.float32,
    )
    keys_f = jnp.dot(
        normed,
        lax.all_gather(key_cols, "row", axis=0, tiled=True),
        preferred_element_type=jnp.float32,
    )
    values_f = jnp.dot(
        normed,
        lax.all_gather(value_cols, "row", axis=0, tiled=True),
        preferred_element_type=jnp.float32,
    )
    positions = row_index * tok_rows + jnp.arange(tok_rows, dtype=jnp.int32)
    cosine, sine = rope_tables(positions, HD)
    q_rot = rotate(queries.reshape(tok_rows, local_heads, HD), cosine, sine).astype(jnp.bfloat16)
    k_rot = (
        rotate(keys_f.reshape(tok_rows, 1, HD), cosine, sine)
        .reshape(tok_rows, HD)
        .astype(jnp.bfloat16)
    )
    v_cast = values_f.astype(jnp.bfloat16)
    doc_ends = running_sums(doc_lengths)
    query_docs = doc_index(positions, doc_ends)
    score_scale = HD ** (-0.5)
    start_state = (
        jnp.full((local_heads, tok_rows), masked_value, jnp.float32),
        jnp.zeros((local_heads, tok_rows), jnp.float32),
        jnp.zeros((local_heads, tok_rows, HD), jnp.float32),
    )
    key_piece = lax.all_gather(k_rot, "row", axis=0, tiled=True)
    value_piece = lax.all_gather(v_cast, "row", axis=0, tiled=True)
    blocks = key_piece.shape[0] // tok_rows
    key_blocks = key_piece.reshape(blocks, tok_rows, HD)
    value_blocks = value_piece.reshape(blocks, tok_rows, HD)

    def visit(state, block_in):
        key_block, value_block, block_number = block_in
        run_max, run_total, run_acc = state
        key_pos = block_number * tok_rows + jnp.arange(tok_rows, dtype=jnp.int32)
        allowed = (query_docs[:, None] == doc_index(key_pos, doc_ends)[None, :]) & (
            key_pos[None, :] <= positions[:, None]
        )
        scores = (
            jnp.einsum("qhd,kd->hqk", q_rot, key_block, preferred_element_type=jnp.float32)
            * score_scale
        )
        masked = jnp.where(allowed[None], scores, masked_value)
        new_max = jnp.maximum(run_max, jnp.max(masked, axis=2))
        factor = jnp.exp(run_max - new_max)
        weights = jnp.where(allowed[None], jnp.exp(masked - new_max[:, :, None]), 0.0)
        new_total = run_total * factor + jnp.sum(weights, axis=2)
        new_acc = run_acc * factor[:, :, None] + jnp.einsum(
            "hqk,kd->hqd",
            weights.astype(jnp.bfloat16),
            value_block,
            preferred_element_type=jnp.float32,
        )
        return ((new_max, new_total, new_acc), None)

    final_state, unused = lax.scan(
        visit, start_state, (key_blocks, value_blocks, jnp.arange(blocks, dtype=jnp.int32))
    )
    run_max, run_total, run_acc = final_state
    context = (
        (run_acc / run_total[:, :, None])
        .astype(jnp.bfloat16)
        .transpose(1, 0, 2)
        .reshape(tok_rows, query_cols)
    )
    weight_whole = lax.all_gather(w_out, "row", axis=0, tiled=True)
    projected = jnp.dot(
        lax.all_gather(context, "col", axis=1, tiled=True),
        weight_whole,
        preferred_element_type=jnp.float32,
    )
    return (tokens.astype(jnp.float32) + projected).astype(jnp.bfloat16)


def solution(mesh):
    rows, cols = mesh.shape["row"], mesh.shape["col"]
    if (rows, cols) == (4, 8):
        body = functools.partial(stationary_body, rows, cols)
    else:
        body = gathered_body
    return jax.shard_map(
        body,
        mesh=mesh,
        in_specs=(
            P("row", "col"),
            P(),
            P("row", "col"),
            P("row", None),
            P("row", None),
            P("row", "col"),
            P(),
        ),
        out_specs=P("row", "col"),
        check_vma=False,
    )
```

```python
import functools

import jax
import jax.numpy as jnp
from jax import lax
from jax.experimental import pallas as pl
from jax.experimental.pallas import tpu as pltpu
from jax.sharding import PartitionSpec as P

HEADS = 64
KVH = 8
HD = 128


rope_base = 500000.0
norm_eps = 1e-05
masked_value = -1e30
f32 = jnp.float32
bf16 = jnp.bfloat16


def rope_tables(positions, head_dim):
    freq_index = jnp.arange(head_dim // 2, dtype=jnp.int32).astype(jnp.float32)
    inverse = rope_base ** (-2.0 * freq_index / head_dim)
    angles = positions.astype(jnp.float32)[:, None] * inverse[None, :]
    return (jnp.cos(angles), jnp.sin(angles))


def rotate(vectors, cosine, sine):
    half_dim = vectors.shape[-1] // 2
    first = vectors[..., :half_dim]
    second = vectors[..., half_dim:]
    cos_part = cosine[:, None, :]
    sin_part = sine[:, None, :]
    return jnp.concatenate(
        [first * cos_part - second * sin_part, second * cos_part + first * sin_part], axis=-1
    )


def running_sums(doc_lengths):
    ends, total = [], jnp.int32(0)
    for i in range(doc_lengths.shape[0]):
        total = total + doc_lengths[i]
        ends.append(total)
    return jnp.stack(ends)


def doc_index(positions, doc_ends):
    return jnp.sum((positions[:, None] >= doc_ends[None, :]).astype(jnp.int32), axis=1)


PARTS = (16, 32, 32)
STEPS = (
    1, 2, 0, 1, 2, 0, 1, 3, 1, 0, 2, 0, 1, 2, 1, 0, 3, 2, 1, 0, 3, 3, 2, 0,
    3, 1, 1, 2, 2, 3, 2, 1, 3, 1, 1, 3, 2, 2, 1, 3, 2, 3, 1, 3, 2, 3, 3, 2,
    3,
)
KEY_BLOCK = 512
VMEM = 56 * 2**20
LESS_VMEM = 24 * 2**20
COST = pl.CostEstimate(flops=1, bytes_accessed=1, transcendentals=0)


def offsets(parts):
    return [sum(parts[:j]) for j in range(len(parts))]


class Order:
    def __init__(self):
        self.last = ()

    def __call__(self, *arrays):
        tied = lax.optimization_barrier((*arrays, *self.last))
        self.last = (tied[0],)
        return tied[0] if len(arrays) == 1 else tied[: len(arrays)]


class Strand:
    def __init__(self, order, steps):
        self.order, self.steps, self.result = order, steps, None
        self.waits = next(steps)

    def step(self):
        try:
            self.waits = self.steps.send(self.order(*self.waits) if self.waits else None)
        except StopIteration as end:
            self.result = end.value


def kv_matmul(share, w_key, w_value, rows):
    tokens, depth = share.shape
    pair = 2 * HD

    def kernel(x_ref, k_ref, v_ref, o_ref):
        o_ref[0, :, :pair] = jnp.dot(x_ref[...], k_ref[...], preferred_element_type=f32)
        o_ref[0, :, pair:] = jnp.dot(x_ref[...], v_ref[...], preferred_element_type=f32)

    return pl.pallas_call(
        kernel,
        grid=(rows,),
        in_specs=[
            pl.BlockSpec((tokens, depth), lambda d: (0, 0)),
            pl.BlockSpec((depth, pair), lambda d: (0, d)),
            pl.BlockSpec((depth, pair), lambda d: (0, d)),
        ],
        out_specs=pl.BlockSpec((1, tokens, 2 * pair), lambda d: (d, 0, 0)),
        out_shape=jax.ShapeDtypeStruct((rows, tokens, 2 * pair), f32),
        compiler_params=pltpu.CompilerParams(vmem_limit_bytes=LESS_VMEM),
        cost_estimate=COST,
        name="kv_matmul",
    )(share, w_key, w_value)


def turn(vectors, cosine, sine):
    return vectors * cosine + pltpu.roll(vectors, HD // 2, 1) * sine


def kv_finish(where, came, part, cosine, sine):
    tokens = came.shape[0]
    pair = 2 * HD

    def kernel(at_ref, came_ref, part_ref, cos_ref, sin_ref, keep_ref, give_ref):
        side = at_ref[1]
        for o_ref, head in ((keep_ref, side), (give_ref, 1 - side)):
            for i in range(2):
                cut = pl.ds(pl.multiple_of(i * pair + head * HD, HD), HD)
                whole = came_ref[:, cut].astype(f32) + part_ref[0, :, cut]
                if i == 0:
                    whole = turn(whole, cos_ref[...], sin_ref[...])
                o_ref[i] = whole.astype(bf16)

    full = lambda i, at: (0, 0)
    out = pl.BlockSpec((2, tokens, HD), lambda i, at: (0, 0, 0))
    return pl.pallas_call(
        kernel,
        grid_spec=pltpu.PrefetchScalarGridSpec(
            num_scalar_prefetch=1,
            grid=(1,),
            in_specs=[
                pl.BlockSpec((tokens, 2 * pair), full),
                pl.BlockSpec((1, tokens, 2 * pair), lambda i, at: (at[0], 0, 0)),
                pl.BlockSpec((tokens, HD), full),
                pl.BlockSpec((tokens, HD), full),
            ],
            out_specs=[out, out],
        ),
        out_shape=[jax.ShapeDtypeStruct((2, tokens, HD), bf16)] * 2,
        compiler_params=pltpu.CompilerParams(vmem_limit_bytes=VMEM),
        cost_estimate=COST,
        name="kv_finish",
    )(where, came, part, cosine, sine)


def kv_assemble(col, pieces, rows, tok_rows, parts):
    cols = len(pieces)
    share = pieces[0].shape[1] // rows

    def kernel(col_ref, *refs):
        o_ref = refs[-1]
        for k in range(cols):
            source = col_ref[0] ^ k
            for t in range(rows):
                for off, size in zip(offsets(parts), parts):
                    first = t * tok_rows + off * cols
                    at = pl.multiple_of(first + source * size, 16)
                    here = t * share + off
                    for i in range(2):
                        o_ref[i, pl.ds(at, size), :] = refs[k][i, here : here + size, :]

    return pl.pallas_call(
        kernel,
        in_specs=[pl.BlockSpec(memory_space=pltpu.SMEM)]
        + [pl.BlockSpec(memory_space=pltpu.VMEM)] * cols,
        out_specs=pl.BlockSpec(memory_space=pltpu.VMEM),
        out_shape=jax.ShapeDtypeStruct((2, rows * tok_rows, HD), bf16),
        compiler_params=pltpu.CompilerParams(vmem_limit_bytes=VMEM),
        cost_estimate=COST,
        name="kv_assemble",
    )(col, *pieces)


def query_matmul(col, pieces, weights, w_query, rows, size):
    pairs = len(pieces)
    cols, depth = 2 * pairs, pieces[0].shape[2]
    group = rows * size
    pair = weights[0].shape[1]
    n = len(weights)

    def kernel(col_ref, *refs):
        x_refs, w_refs = refs[:pairs], refs[pairs : pairs + n]
        own_ref, o_ref, xs, ws, x_sem, w_sem = refs[pairs + n :]
        m = pl.program_id(0)
        col = col_ref[0]

        @pl.when(m == 0)
        def _():
            copies = []
            for i, both in enumerate(source_of(col)):
                for h, source in enumerate(both):
                    at = pl.multiple_of(source * group, group)
                    copies.append(
                        pltpu.make_async_copy(
                            x_refs[i].at[h], xs.at[pl.ds(at, group), :], x_sem.at[2 * i + h]
                        )
                    )
            for copy in copies:
                copy.start()
            for i in range(n):
                held = (col // 2 + i) % n
                stays = col == 4 * (col % 2) + held
                cut = pl.ds(pl.multiple_of(held * pair, pair), pair)

                @pl.when(stays)
                def _(i=i, cut=cut):
                    pltpu.make_async_copy(own_ref.at[:, cut], ws.at[i], w_sem.at[i]).start()

                @pl.when(jnp.logical_not(stays))
                def _(i=i):
                    pltpu.make_async_copy(w_refs[i], ws.at[i], w_sem.at[i]).start()

            for copy in copies:
                copy.wait()

        pltpu.make_async_copy(w_refs[0], ws.at[m], w_sem.at[m]).wait()

        total = jnp.dot(xs[...], ws[m], preferred_element_type=f32)
        for c in range(cols):
            for t in range(rows):
                first = (c * rows + t) * size
                o_ref[0, t, c * size : (c + 1) * size, :] = total[first : first + size, :]

    return pl.pallas_call(
        kernel,
        grid=(n,),
        in_specs=[pl.BlockSpec(memory_space=pltpu.SMEM)]
        + [pl.BlockSpec(memory_space=pl.ANY)] * (pairs + n + 1),
        out_specs=pl.BlockSpec((1, rows, cols * size, pair), lambda m: (m, 0, 0, 0)),
        out_shape=jax.ShapeDtypeStruct((n, rows, cols * size, pair), f32),
        scratch_shapes=[
            pltpu.VMEM((cols * group, depth), bf16),
            pltpu.VMEM((n, depth, pair), bf16),
            pltpu.SemaphoreType.DMA((cols,)),
            pltpu.SemaphoreType.DMA((n,)),
        ],
        compiler_params=pltpu.CompilerParams(vmem_limit_bytes=VMEM),
        cost_estimate=COST,
        name="query_matmul",
    )(col, *pieces, *weights, w_query)


def attention_kernel(first_of, tok_rows, at_ref, ends_ref, came_ref, part_ref, cos_ref, sin_ref, k_ref, v_ref, o_ref):
    docs = ends_ref.shape[0]
    size = came_ref.shape[1]
    first = pl.program_id(0) * tok_rows + first_of
    heads = []
    for h in range(2):
        cut = slice(h * HD, (h + 1) * HD)
        whole = came_ref[0, :, cut].astype(f32) + part_ref[0, 0, :, cut]
        heads.append(turn(whole, cos_ref[...], sin_ref[...]).astype(bf16))
    queries = jnp.concatenate(heads, axis=0)
    row = lax.broadcasted_iota(jnp.int32, (2 * size, 1), 0)
    pos = first + jnp.where(row >= size, row - size, row)
    start = jnp.zeros_like(pos)
    low = jnp.int32(0)
    for e in range(docs - 1):
        end = ends_ref[e]
        start = jnp.where(pos >= end, end, start)
        low = jnp.where(first >= end, end, low)
    scale = HD ** (-0.5)

    def visit(block, state):
        run_max, run_total, run_acc = state
        at = pl.multiple_of(block * KEY_BLOCK, KEY_BLOCK)
        keys = k_ref[0, pl.ds(at, KEY_BLOCK), :]
        values = v_ref[0, pl.ds(at, KEY_BLOCK), :]
        scores = lax.dot_general(
            queries, keys, (((1,), (1,)), ((), ())), preferred_element_type=f32
        )
        key_pos = at + lax.broadcasted_iota(jnp.int32, (1, KEY_BLOCK), 1)
        allowed = (key_pos <= pos) & (key_pos >= start)
        masked = jnp.where(allowed, scores, masked_value)
        new_max = jnp.maximum(run_max, jnp.max(masked, axis=1, keepdims=True))
        factor = jnp.exp((run_max - new_max) * scale)
        weights = jnp.where(allowed, jnp.exp((masked - new_max) * scale), 0.0)
        new_total = run_total * factor + jnp.sum(weights, axis=1, keepdims=True)
        new_acc = run_acc * factor + jnp.dot(
            weights.astype(bf16), values, preferred_element_type=f32
        )
        return new_max, new_total, new_acc

    state = (
        jnp.full((2 * size, 1), masked_value, f32),
        jnp.zeros((2 * size, 1), f32),
        jnp.zeros((2 * size, HD), f32),
    )
    last = (first + size - 1) // KEY_BLOCK + 1
    run_max, run_total, run_acc = lax.fori_loop(low // KEY_BLOCK, last, visit, state)
    context = (run_acc / run_total).astype(bf16)
    o_ref[0, :, :HD] = context[:size]
    o_ref[0, :, HD:] = context[size:]


def attend(which, came, part, cosine, sine, kv, doc_ends, first_of, tok_rows):
    rows, size, pair = came.shape
    total = kv.shape[1]
    table = pl.BlockSpec((size, HD), lambda g, at, ends: (g, 0))
    return pl.pallas_call(
        functools.partial(attention_kernel, first_of, tok_rows),
        grid_spec=pltpu.PrefetchScalarGridSpec(
            num_scalar_prefetch=2,
            grid=(rows,),
            in_specs=[
                pl.BlockSpec((1, size, pair), lambda g, at, ends: (g, 0, 0)),
                pl.BlockSpec((1, 1, size, pair), lambda g, at, ends: (at[0], g, 0, 0)),
                table,
                table,
                pl.BlockSpec((1, total, HD), lambda g, at, ends: (0, 0, 0)),
                pl.BlockSpec((1, total, HD), lambda g, at, ends: (1, 0, 0)),
            ],
            out_specs=pl.BlockSpec((1, size, pair), lambda g, at, ends: (g, 0, 0)),
        ),
        out_shape=jax.ShapeDtypeStruct((rows, size, pair), bf16),
        compiler_params=pltpu.CompilerParams(vmem_limit_bytes=LESS_VMEM),
        cost_estimate=COST,
        name="attend",
    )(which, doc_ends, came, part, cosine, sine, kv, kv)


def out_matmul(col, pieces, w_out, rows):
    pairs = len(pieces)
    pair = pieces[0].shape[2]
    size = pieces[0].shape[1] // rows
    depth, width = w_out.shape

    def kernel(col_ref, *refs):
        x_refs, (w_ref, o_ref, xs) = refs[:pairs], refs[pairs:]
        for i, both in enumerate(source_of(col_ref[0])):
            for h, source in enumerate(both):
                at = pl.multiple_of(source * pair, pair)
                xs[:, pl.ds(at, pair)] = x_refs[i][h]
        o_ref[0] = jnp.dot(xs[...], w_ref[...], preferred_element_type=f32)

    return pl.pallas_call(
        kernel,
        grid=(rows,),
        in_specs=[pl.BlockSpec(memory_space=pltpu.SMEM)]
        + [pl.BlockSpec((2, size, pair), lambda t: (0, t, 0))] * pairs
        + [pl.BlockSpec((depth, width), lambda t: (0, 0))],
        out_specs=pl.BlockSpec((1, size, width), lambda t: (t, 0, 0)),
        out_shape=jax.ShapeDtypeStruct((rows, size, width), f32),
        scratch_shapes=[pltpu.VMEM((size, depth), bf16)],
        compiler_params=pltpu.CompilerParams(vmem_limit_bytes=LESS_VMEM),
        cost_estimate=COST,
        name="out_matmul",
    )(col, *pieces, w_out)


def plane_gather(order, own, cols):
    def send(x, even, odd):
        return lax.ppermute(x, "col", [(i, i ^ (odd if i % 2 else even)) for i in range(cols)])

    first = yield (send(own, 2, 4),)
    two = order(jnp.stack([own, first]))
    beside = send(two, 1, 1)
    second = yield (send(two, 4, 2),)
    across, beside = yield (send(second, 1, 1), beside)
    return [two, second, beside, across]


def source_of(col):
    a = 2 + 2 * (col % 2)
    return [[col ^ k for k in ks] for ks in ((0, a), (6 - a, 6), (1, 7 - a), (a ^ 1, 7))]


def ring(order, part_of, row_index, rows):
    onward = [(i, (i + 1) % rows) for i in range(rows)]
    total = part_of((row_index - 1) % rows).astype(bf16)
    for step in range(1, rows):
        came = yield (lax.ppermute(order(total), "row", onward),)
        total = came.astype(f32) + part_of((row_index - 1 - step) % rows)
        total = total.astype(bf16)
    return came


def stationary_body(rows, cols, tokens, norm_gain, w_query, w_key, w_value, w_out, doc_lengths):
    tok_rows, feats = tokens.shape
    col = lax.axis_index("col")
    row = lax.axis_index("row")
    col_at = col[None].astype(jnp.int32)
    depth = w_query.shape[0]
    share_rows = tok_rows // cols
    parts = PARTS
    starts = offsets(parts)
    pair = 2 * HD
    doc_ends = running_sums(doc_lengths)

    order = Order()
    spread = jnp.concatenate(
        [
            tokens[a * cols : (a + p) * cols].reshape(cols, p, feats)
            for a, p in zip(starts, parts)
        ],
        axis=1,
    )
    mine = lax.all_to_all(order(spread), "col", 0, 0)

    w_pieces = []
    for m in range(cols // 2):
        which = (col // 2 + m) % (cols // 2)
        w_pieces.append(lax.dynamic_slice_in_dim(w_query, which * pair, pair, 1))
    w_pieces = list(order(*w_pieces))
    for m in range(cols // 2):
        moves = [(i, 4 * (i % 2) + (i // 2 + m) % 4) for i in range(cols)]
        moves = [(i, to) for i, to in moves if i != to]
        w_pieces[m] = lax.ppermute(w_pieces[m], "col", moves)

    positions = jnp.arange(rows * tok_rows, dtype=jnp.int32)
    cosine, sine = rope_tables(positions, HD)
    cos_all = jnp.concatenate([cosine, cosine], axis=1).reshape(rows, tok_rows, HD)
    sin_all = jnp.concatenate([-sine, sine], axis=1).reshape(rows, tok_rows, HD)

    def of_mine(table):
        return jnp.concatenate(
            [
                lax.dynamic_slice_in_dim(table, a * cols + col * p, p, 1)
                for a, p in zip(starts, parts)
            ],
            axis=1,
        ).reshape(-1, HD)

    tables = [of_mine(cos_all), of_mine(sin_all)]
    for a, p in zip(starts, parts):
        tables += [t[:, a * cols : (a + p) * cols].reshape(-1, HD) for t in (cos_all, sin_all)]
    tables = order(*tables)

    mine = order(mine).astype(f32)
    rms = lax.rsqrt(jnp.mean(mine * mine, axis=(0, 2), keepdims=True) + norm_eps)
    gain = norm_gain.astype(f32).reshape(cols, 1, feats)
    normed = (mine * rms * gain).astype(bf16)
    normed = normed.reshape(rows, cols // rows, share_rows, feats).transpose(0, 2, 1, 3)
    normed = normed.reshape(rows, share_rows, depth)
    share = lax.all_to_all(order(normed), "row", 0, 0)

    share = order(share)

    where = jnp.stack([row, col // 4]).astype(jnp.int32)
    which = ((col % 4 - row) % rows)[None].astype(jnp.int32)

    def keys_and_values():
        part = kv_matmul(share.reshape(-1, depth), w_key, w_value, rows)
        came = yield from ring(
            order, lambda d: lax.dynamic_index_in_dim(part, d, 0, keepdims=False), row, rows
        )
        keep, give = order(*kv_finish(where, came, part, tables[0], tables[1]))
        pieces = {0: keep}
        pieces[4] = yield (lax.ppermute(give, "col", [(i, i ^ 4) for i in range(cols)]),)
        for bit in (2, 1):
            together = order(jnp.stack(list(pieces.values())))
            came = yield (lax.ppermute(together, "col", [(i, i ^ bit) for i in range(cols)]),)
            for i, k in enumerate(list(pieces)):
                pieces[k ^ bit] = came[i]
        return order(
            kv_assemble(col_at, [pieces[k] for k in range(cols)], rows, tok_rows, parts)
        )

    def chunk(j):
        a, p = starts[j], parts[j]
        own = order(share[:, a : a + p].reshape(rows * p, depth))
        pieces = yield from plane_gather(order, own, cols)
        q_part = query_matmul(col_at, pieces, w_pieces, w_query, rows, p)
        came = yield from ring(
            order,
            lambda d: lax.dynamic_index_in_dim(q_part, (col % 4 - d) % rows, 0, keepdims=False),
            row,
            rows,
        )
        yield ()
        context = attend(
            which, came, q_part, *tables[2 + 2 * j : 4 + 2 * j], strands[0].result, doc_ends, a * cols, tok_rows
        )
        context = order(context.reshape(rows * p * cols, pair))
        pieces = yield from plane_gather(order, context, cols)
        o_part = out_matmul(col_at, pieces, w_out, rows)
        came = yield from ring(
            order, lambda d: lax.dynamic_index_in_dim(o_part, d, 0, keepdims=False), row, rows
        )
        own = lax.dynamic_index_in_dim(o_part, row, 0, keepdims=False)
        mine = tokens[a * cols : (a + p) * cols].astype(f32)
        return order((mine + (came.astype(f32) + own)).astype(bf16))

    strands = {}
    for n, i in enumerate(STEPS):
        if n == 2:
            w_pieces = list(order(*w_pieces))
        if i in strands:
            strands[i].step()
        else:
            strands[i] = Strand(order, chunk(i - 1) if i else keys_and_values())
    return jnp.concatenate([strands[j + 1].result for j in range(len(parts))], axis=0)


def gathered_body(tokens, norm_gain, w_query, w_key, w_value, w_out, doc_lengths):
    tok_rows = tokens.shape[0]
    col_index = lax.axis_index("col")
    row_index = lax.axis_index("row")
    query_cols = w_query.shape[1]
    local_heads = query_cols // HD
    group_size = HEADS // KVH
    kv_head = col_index * local_heads // group_size
    key_cols = lax.dynamic_slice_in_dim(w_key, kv_head * HD, HD, 1)
    value_cols = lax.dynamic_slice_in_dim(w_value, kv_head * HD, HD, 1)
    gathered = lax.all_gather(tokens, "col", axis=1, tiled=True)
    whole_f = gathered.astype(jnp.float32)
    whole_rms = lax.rsqrt(jnp.mean(whole_f * whole_f, axis=1, keepdims=True) + norm_eps)
    normed = (whole_f * whole_rms * norm_gain.astype(jnp.float32)[None, :]).astype(jnp.bfloat16)
    queries = jnp.dot(
        normed,
        lax.all_gather(w_query, "row", axis=0, tiled=True),
        preferred_element_type=jnp.float32,
    )
    keys_f = jnp.dot(
        normed,
        lax.all_gather(key_cols, "row", axis=0, tiled=True),
        preferred_element_type=jnp.float32,
    )
    values_f = jnp.dot(
        normed,
        lax.all_gather(value_cols, "row", axis=0, tiled=True),
        preferred_element_type=jnp.float32,
    )
    positions = row_index * tok_rows + jnp.arange(tok_rows, dtype=jnp.int32)
    cosine, sine = rope_tables(positions, HD)
    q_rot = rotate(queries.reshape(tok_rows, local_heads, HD), cosine, sine).astype(jnp.bfloat16)
    k_rot = (
        rotate(keys_f.reshape(tok_rows, 1, HD), cosine, sine)
        .reshape(tok_rows, HD)
        .astype(jnp.bfloat16)
    )
    v_cast = values_f.astype(jnp.bfloat16)
    doc_ends = running_sums(doc_lengths)
    query_docs = doc_index(positions, doc_ends)
    score_scale = HD ** (-0.5)
    start_state = (
        jnp.full((local_heads, tok_rows), masked_value, jnp.float32),
        jnp.zeros((local_heads, tok_rows), jnp.float32),
        jnp.zeros((local_heads, tok_rows, HD), jnp.float32),
    )
    key_piece = lax.all_gather(k_rot, "row", axis=0, tiled=True)
    value_piece = lax.all_gather(v_cast, "row", axis=0, tiled=True)
    blocks = key_piece.shape[0] // tok_rows
    key_blocks = key_piece.reshape(blocks, tok_rows, HD)
    value_blocks = value_piece.reshape(blocks, tok_rows, HD)

    def visit(state, block_in):
        key_block, value_block, block_number = block_in
        run_max, run_total, run_acc = state
        key_pos = block_number * tok_rows + jnp.arange(tok_rows, dtype=jnp.int32)
        allowed = (query_docs[:, None] == doc_index(key_pos, doc_ends)[None, :]) & (
            key_pos[None, :] <= positions[:, None]
        )
        scores = (
            jnp.einsum("qhd,kd->hqk", q_rot, key_block, preferred_element_type=jnp.float32)
            * score_scale
        )
        masked = jnp.where(allowed[None], scores, masked_value)
        new_max = jnp.maximum(run_max, jnp.max(masked, axis=2))
        factor = jnp.exp(run_max - new_max)
        weights = jnp.where(allowed[None], jnp.exp(masked - new_max[:, :, None]), 0.0)
        new_total = run_total * factor + jnp.sum(weights, axis=2)
        new_acc = run_acc * factor[:, :, None] + jnp.einsum(
            "hqk,kd->hqd",
            weights.astype(jnp.bfloat16),
            value_block,
            preferred_element_type=jnp.float32,
        )
        return ((new_max, new_total, new_acc), None)

    final_state, unused = lax.scan(
        visit, start_state, (key_blocks, value_blocks, jnp.arange(blocks, dtype=jnp.int32))
    )
    run_max, run_total, run_acc = final_state
    context = (
        (run_acc / run_total[:, :, None])
        .astype(jnp.bfloat16)
        .transpose(1, 0, 2)
        .reshape(tok_rows, query_cols)
    )
    weight_whole = lax.all_gather(w_out, "row", axis=0, tiled=True)
    projected = jnp.dot(
        lax.all_gather(context, "col", axis=1, tiled=True),
        weight_whole,
        preferred_element_type=jnp.float32,
    )
    return (tokens.astype(jnp.float32) + projected).astype(jnp.bfloat16)


def solution(mesh):
    rows, cols = mesh.shape["row"], mesh.shape["col"]
    if (rows, cols) == (4, 8):
        body = functools.partial(stationary_body, rows, cols)
    else:
        body = gathered_body
    return jax.shard_map(
        body,
        mesh=mesh,
        in_specs=(
            P("row", "col"),
            P(),
            P("row", "col"),
            P("row", None),
            P("row", None),
            P("row", "col"),
            P(),
        ),
        out_specs=P("row", "col"),
        check_vma=False,
    )
```
